128 devices in a mesh: grid: 16 (over z, x_hi, core), rec: 8 (over y, x_lo).
Axes of the slice: x: 4 (x_hi: 2, x_lo: 2; x = x_hi * 2 + x_lo), y: 4, z: 4, core: 2. Of those that a mesh axis runs over, the one named last changes fastest.
Arguments:
- adjoint: float32 [4096, 128, 256], P('rec', 'grid'), may hold values from -26 to 26, as said below
- courant: float32 [4, 128, 256], P(None, 'grid'), may hold values from 0.02 to 0.22
- detector: int32 [4096], P('rec'), may hold values from 0 to 32767
- sources: int32 [32768], P('grid'), may hold values from 0 to 32767, as said below
- emission: float32 [32768], P('grid'), may hold values from 0.3 to 3
Outputs:
- advanced: float32 [4096, 128, 256], P('rec', 'grid')
- gram: float32 [4096, 4096], P('grid', 'rec')
The draws below stay inside these ranges and needn't reach their ends.
Inputs may be any that keep to these rules, and one draw needn't show every extreme that they name: `adjoint`: each receptor's field is rough from cell to cell; the fields of different receptors need not be independent of one another. The sources of the j-th run of 2048 entries are distinct cells of grid rows j * 8 to (j + 1) * 8 - 1, so each run is an ordering of all cells of those rows.
All inputs are finite; a program needn't handle non-finite values.
Results may differ from the reference program's by a relative error of at most 0.0008.
Values may be sent and summed in bfloat16 or wider, within the bound.
No kernel may reach another device: no remote copies, remote signals or barrier semaphores. Data moves between devices by JAX's collectives and lax.ppermute only.
A program may use at most 128 MiB of HBM per device.

```python
import math
import jax
import jax.numpy as jnp
from jax import lax

RG = 512
CX = 8
NY = 256
SRC_DEV = 2048
STEPS = 2
R = 4096
NX = 128
SOURCES = 32768
N_GRID = 16
N_REC = 8


def draw_adjoint(key, part):
    first, second, third = jax.random.split(key, 3)
    base = jax.random.truncated_normal(first, -4.0, 4.0, (R, NX, NY), jnp.float32)
    common = jax.random.truncated_normal(second, -4.0, 4.0, (NX, NY), jnp.float32)
    weight = jax.random.uniform(third, (R,), jnp.float32, 0.1, 0.3)
    return base + weight[:, None, None] * common[None, :, :]


def draw_sources(key, part):
    cells = CX * NY
    tile_keys = jax.random.split(jax.random.fold_in(key, 17), N_GRID)
    inner = jax.vmap(lambda tile_key: jax.random.permutation(tile_key, cells - 2))(tile_keys)
    inner = (inner[:, :SRC_DEV - 2] + 1).astype(jnp.int32)
    first_cell = jnp.zeros((N_GRID, 1), jnp.int32)
    last_cell = jnp.full((N_GRID, 1), cells - 1, jnp.int32)
    offsets = jnp.concatenate([first_cell, inner, last_cell], axis=1)
    starts = jnp.arange(N_GRID, dtype=jnp.int32)[:, None] * cells
    return (starts + offsets).reshape(-1).astype(jnp.int32)


def place_ends(values, own_key, smallest, top_value):
    longest = values.shape.index(max(values.shape))
    spots = []
    for shift in (0, 1):
        where = [jax.random.randint(jax.random.fold_in(own_key, axis), (), 0, length) for axis, length in enumerate(values.shape)]
        where[longest] = (where[longest] + shift) % values.shape[longest]
        spots.append(tuple(where))
    return values.at[spots[0]].set(smallest).at[spots[1]].set(top_value)


def shard_levels(own_key, shape, cuts, least, largest):
    level, own = 1.0, jax.random.fold_in(own_key, 6)
    for axis_at, shards_of in cuts:
        heights = jnp.exp(jax.random.uniform(jax.random.fold_in(own, axis_at), (shards_of,), jnp.float32, least / len(cuts), largest / len(cuts)))
        level = level * jnp.repeat(heights, shape[axis_at] // shards_of).reshape([-1 if axis == axis_at else 1 for axis in range(len(shape))])
    return level


def setup_inputs(seed: int = 0) -> dict:
    streams_of = jax.random.split(jax.random.key(seed), 6)
    return {
        "adjoint": draw_adjoint(jax.random.fold_in(streams_of[5], 71), 0),
        "courant": jnp.clip(0.02 + 0.2 * jax.random.uniform(streams_of[1], (4, NX, NY), jnp.float32) ** shard_levels(streams_of[1], (4, NX, NY), ((1, 16),), -0.2, 0.2), 0.02, 0.22),
        "detector": place_ends(jax.random.randint(streams_of[2], (R,), 0, NX * NY), jax.random.fold_in(streams_of[2], 1), 0, (NX * NY) - 1).astype(jnp.int32),
        "sources": draw_sources(jax.random.fold_in(streams_of[5], 71), 0),
        "emission": jnp.clip(jnp.exp(math.log(3.0) - 2.3025851 * jax.random.uniform(streams_of[4], (SOURCES,), jnp.float32) ** shard_levels(streams_of[4], (SOURCES,), ((0, 16),), -0.2, 0.2)), 0.3, 3.0),
    }


def advance(field, coef, detect):
    count = field.shape[0]
    padded = jnp.pad(field, ((0, 0), (1, 1), (1, 1)))
    north = padded[:, 2:, 1:-1]
    south = padded[:, :-2, 1:-1]
    east = padded[:, 1:-1, 2:]
    west = padded[:, 1:-1, :-2]
    fresh = field + coef[0] * (north - field) + coef[1] * (south - field) + coef[2] * (east - field) + coef[3] * (west - field)
    flat = fresh.reshape(count, -1).at[jnp.arange(count), detect].add(jnp.float32(1.0))
    return flat.reshape(field.shape)


def reference(adjoint, courant, detector, sources, emission):
    fields = adjoint.reshape(N_REC, RG, NX, NY)
    detects = detector.reshape(N_REC, RG)

    def one_group(pair):
        field, detect = pair
        for step in range(STEPS):
            field = advance(field, courant, detect)
        picked = jnp.take(field.reshape(RG, NX * NY), sources, axis=1)
        return field, (picked * emission[None, :]).astype(jnp.bfloat16)

    finals, footprint = lax.map(one_group, (fields, detects))
    wide = footprint.reshape(R, SOURCES).astype(jnp.float32)
    gram = jnp.dot(wide, wide.T, precision=lax.Precision.HIGHEST, preferred_element_type=jnp.float32) / jnp.float32(SOURCES)
    return finals.reshape(R, NX, NY), gram
```

```python
import jax
import jax.numpy as jnp
from jax import lax
from jax.experimental import pallas as pl
from jax.experimental.pallas import tpu as pltpu
from jax.sharding import Mesh, PartitionSpec as P

GRID = ("z", "xh", "core")
PLANE = ("z", "xh", "xl")
BF = jnp.bfloat16
VMEM_LIMIT = 48 * 1024 * 1024


def swap(axis):
    return [(0, 1), (1, 0)]


def edge_kernel(x_ref, top_ref, bot_ref):
    top_ref[0] = x_ref[:, 0, :].astype(BF)
    top_ref[1] = x_ref[:, 1, :].astype(BF)
    bot_ref[0] = x_ref[:, 6, :].astype(BF)
    bot_ref[1] = x_ref[:, 7, :].astype(BF)


def edges(field):
    groups, rows, width = field.shape
    block = 64
    shape = jax.ShapeDtypeStruct((2, groups, width), BF)
    spec = pl.BlockSpec((2, block, width), lambda i: (0, i, 0))
    return pl.pallas_call(
        edge_kernel,
        grid=(groups // block,),
        in_specs=[pl.BlockSpec((block, rows, width), lambda i: (i, 0, 0))],
        out_specs=[spec, spec],
        out_shape=[shape, shape],
        compiler_params=pltpu.CompilerParams(vmem_limit_bytes=VMEM_LIMIT),
    )(field)


def stencil_kernel(info, x_ref, up_ref, down_ref, coef_ref, emis_ref, det_ref, adv_ref, keep_ref, send_ref):
    block = x_ref.shape[0]
    width = x_ref.shape[2]
    own_first = info[1] == 0
    first_cell = info[2]

    def group(g, carry):
        at = pl.ds(pl.multiple_of(g * 16, 16), 16)
        delta = det_ref[at, :] - first_cell - lax.broadcasted_iota(jnp.int32, (16, width), 1)

        def value(r):
            if r < 0:
                return up_ref[r + 2, at, :].astype(jnp.float32)
            if r > 7:
                return down_ref[r - 8, at, :].astype(jnp.float32)
            return x_ref[at, r, :]

        def step(r, south, center, north):
            east = pltpu.roll(center, width - 1, 1)
            west = pltpu.roll(center, 1, 1)
            c = [coef_ref[k, r + 1:r + 2, :] for k in range(5)]
            pulse = jnp.where(delta == r * width, 1.0, 0.0)
            return c[4] * center + c[0] * north + c[1] * south + c[2] * east + c[3] * west + pulse

        v = {r: value(r) for r in (-2, -1)}
        first = {}
        prints = {}
        for r in range(-1, 9):
            v[r + 1] = value(r + 1)
            first[r] = step(r, v[r - 1], v[r], v[r + 1])
            if r >= 1:
                q = r - 1
                out = step(q, first[q - 1], first[q], first[q + 1])
                adv_ref[at, q, :] = out
                prints[q] = (out * emis_ref[q:q + 1, :])
                if q >= 4:
                    p = q - 4
                    cols = pl.ds(p * width, width)
                    keep_ref[at, cols] = jnp.where(own_first, prints[p], prints[q]).astype(BF)
                    send_ref[at, cols] = jnp.where(own_first, prints[q], prints[p]).astype(BF)
        return carry

    lax.fori_loop(0, block // 16, group, 0)


def stencil(info, field, up, down, coef, emis, det):
    groups, rows, width = field.shape
    block = 64
    count = groups // block
    half = count // 2

    def turned(i, info):
        return lax.rem(i + info[0] * half, count)

    cells = rows * width // 2
    return pl.pallas_call(
        stencil_kernel,
        grid_spec=pltpu.PrefetchScalarGridSpec(
            num_scalar_prefetch=1,
            grid=(count,),
            in_specs=[
                pl.BlockSpec((block, rows, width), lambda i, info: (turned(i, info), 0, 0)),
                pl.BlockSpec((2, block, width), lambda i, info: (0, turned(i, info), 0)),
                pl.BlockSpec((2, block, width), lambda i, info: (0, turned(i, info), 0)),
                pl.BlockSpec((5, rows + 2, width), lambda i, info: (0, 0, 0)),
                pl.BlockSpec((rows, width), lambda i, info: (0, 0)),
                pl.BlockSpec((block, 1), lambda i, info: (turned(i, info), 0)),
            ],
            out_specs=[
                pl.BlockSpec((block, rows, width), lambda i, info: (turned(i, info), 0, 0)),
                pl.BlockSpec((block, cells), lambda i, info: (i, 0)),
                pl.BlockSpec((block, cells), lambda i, info: (i, 0)),
            ],
        ),
        out_shape=[
            jax.ShapeDtypeStruct(field.shape, jnp.float32),
            jax.ShapeDtypeStruct((groups, cells), BF),
            jax.ShapeDtypeStruct((groups, cells), BF),
        ],
        compiler_params=pltpu.CompilerParams(vmem_limit_bytes=VMEM_LIMIT),
    )(info, field, up, down, coef, emis, det)


def gram_kernel(info, a0, a1, a2, a3, o_ref, os_ref, q_ref, qs_ref, out_ref):
    i = pl.program_id(0)
    core, xl, y = info[0], info[1], info[3]
    half = o_ref.shape[1]
    rows = a0.shape[1]
    for d, a_ref in enumerate((a0, a1, a2, a3)):
        for j, (b_own, b_sib) in enumerate(((o_ref, os_ref), (q_ref, qs_ref))):
            slot = lax.rem(y + d, 4) * 4 + lax.rem(i + xl, 2) * 2 + lax.rem(j + xl, 2)
            for m in range(2):
                mine = pl.ds(m * rows, rows)
                sib = pl.ds((1 - m) * rows, rows)
                dims = (((1,), (1,)), ((), ()))
                total = lax.dot_general(
                    a_ref[0, :, :half], b_own[mine, :], dims, preferred_element_type=jnp.float32
                ) + lax.dot_general(
                    a_ref[0, :, half:], b_sib[sib, :], dims, preferred_element_type=jnp.float32
                )
                cols = pl.ds(pl.multiple_of(lax.rem(core + m, 2) * rows, rows), rows)
                out_ref[slot, :, cols] = total.astype(BF)


def partial_gram(info, lefts, rights):
    rows = lefts[0].shape[1]
    depth = lefts[0].shape[2]
    cols = rights[0].shape[0]
    left = pl.BlockSpec((1, rows, depth), lambda i, info: (i, 0, 0))
    right = pl.BlockSpec(rights[0].shape, lambda i, info: (0, 0))
    return pl.pallas_call(
        gram_kernel,
        grid_spec=pltpu.PrefetchScalarGridSpec(
            num_scalar_prefetch=1,
            grid=(2,),
            in_specs=[left] * 4 + [right] * 4,
            out_specs=pl.BlockSpec((16, rows, cols), lambda i, info: (0, 0, 0)),
        ),
        out_shape=jax.ShapeDtypeStruct((16, rows, cols), BF),
        compiler_params=pltpu.CompilerParams(vmem_limit_bytes=VMEM_LIMIT),
    )(info, *lefts, *rights)


def body(adjoint, courant, detector, sources, emission):
    groups, rows, width = adjoint.shape
    core = lax.axis_index("core")
    xl = lax.axis_index("xl")
    y = lax.axis_index("y")
    tile = lax.axis_index(GRID)
    first_cell = tile * rows * width
    info = jnp.stack([core, xl, first_cell, y]).astype(jnp.int32)

    count = lax.axis_size(GRID)
    forward = [(i, i + 1) for i in range(count - 1)]
    backward = [(i + 1, i) for i in range(count - 1)]
    top, bottom = edges(adjoint)
    up = lax.ppermute(bottom, GRID, forward)
    down = lax.ppermute(top, GRID, backward)
    coef_up = lax.ppermute(courant[:, rows - 1:], GRID, forward)
    coef_down = lax.ppermute(courant[:, :1], GRID, backward)
    coef = jnp.concatenate([coef_up, courant, coef_down], axis=1)
    columns = jnp.arange(width)
    coef = jnp.stack([
        coef[0],
        coef[1],
        jnp.where(columns == width - 1, 0.0, coef[2]),
        jnp.where(columns == 0, 0.0, coef[3]),
        1.0 - (coef[0] + coef[1] + coef[2] + coef[3]),
    ])

    local = sources - first_cell
    by_row = jnp.where(
        (local // width)[None, :] == jnp.arange(rows)[:, None], emission[None, :], 0.0
    )
    by_col = ((local % width)[:, None] == columns[None, :]).astype(jnp.float32)
    emis = jnp.dot(by_row, by_col, precision=lax.Precision.HIGHEST)

    field, keep, send = stencil(info, adjoint, up, down, coef, emis, detector[:, None])

    part = groups // 2
    other = lax.ppermute(send, "xl", swap("xl"))
    keep_s = lax.ppermute(keep, "core", swap("core"))
    other_s = lax.ppermute(other, "core", swap("core"))
    own = jnp.stack([
        jnp.concatenate([keep[:part], keep_s[part:]], axis=1),
        jnp.concatenate([other[:part], other_s[part:]], axis=1),
    ])
    lefts = [own] + [
        lax.ppermute(own, "y", [((i + d) % 4, i) for i in range(4)]) for d in (1, 2, 3)
    ]
    partial = partial_gram(info, lefts, (keep, keep_s, other, other_s))
    pieces = lax.all_to_all(partial, PLANE, 0, 0, tiled=True)
    total_sources = sources.shape[0] * count
    gram = jnp.sum(pieces.astype(jnp.float32), axis=0) / jnp.float32(total_sources)
    return field, gram


def solution(mesh):
    fine = Mesh(mesh.devices.reshape(4, 2, 2, 4, 2), ("z", "xh", "core", "y", "xl"))
    rec = ("y", "xl")
    in_specs = (P(rec, GRID, None), P(None, GRID, None), P(rec), P(GRID), P(GRID))
    out_specs = (P(rec, GRID, None), P(GRID, rec))
    return jax.shard_map(body, mesh=fine, in_specs=in_specs, out_specs=out_specs, check_vma=False)
```

```python
import jax
import jax.numpy as jnp
from jax import lax
from jax.experimental import pallas as pl
from jax.experimental.pallas import tpu as pltpu
from jax.sharding import Mesh, PartitionSpec as P

GRID = ("z", "xh", "core")
PLANE = ("z", "xh", "xl")
BF = jnp.bfloat16
VMEM_LIMIT = 40 * 1024 * 1024
LIFT = 1.0 / 256
SWAP = [(0, 1), (1, 0)]


def params():
    return pltpu.CompilerParams(vmem_limit_bytes=VMEM_LIMIT)


def cost(flops, moved):
    return pl.CostEstimate(flops=flops, bytes_accessed=moved, transcendentals=0)


def edge_kernel(x_ref, top_ref, bot_ref):
    top_ref[0] = x_ref[:, 0, :].astype(BF)
    top_ref[1] = x_ref[:, 1, :].astype(BF)
    bot_ref[0] = x_ref[:, 6, :].astype(BF)
    bot_ref[1] = x_ref[:, 7, :].astype(BF)


def edges(field):
    groups, rows, width = field.shape
    block = 64
    shape = jax.ShapeDtypeStruct((2, groups, width), BF)
    spec = pl.BlockSpec((2, block, width), lambda i: (0, i, 0))
    return pl.pallas_call(
        edge_kernel,
        grid=(groups // block,),
        in_specs=[pl.BlockSpec((block, rows, width), lambda i: (i, 0, 0))],
        out_specs=[spec, spec],
        out_shape=[shape, shape],
        cost_estimate=cost(1000, 6 << 20),
        compiler_params=params(),
    )(field)


def stepper(coef_ref, offset, delta, width):
    def step(r, south, center, north):
        east = pltpu.roll(center, width - 1, 1)
        west = pltpu.roll(center, 1, 1)
        at = r + offset
        c = [coef_ref[k, at:at + 1, :] for k in range(5)]
        pulse = jnp.where(delta == r * width, 1.0, 0.0)
        return c[4] * center + c[0] * north + c[1] * south + c[2] * east + c[3] * west + pulse

    return step


def offsets(det_ref, at, first_cell, width):
    return det_ref[at, :] - first_cell - lax.broadcasted_iota(jnp.int32, (16, width), 1)


def put(keep_ref, send_ref, at, p, own_first, low, high):
    width = low.shape[1]
    cols = pl.ds(p * width, width)
    keep_ref[at, cols] = jnp.where(own_first, low, high).astype(BF)
    send_ref[at, cols] = jnp.where(own_first, high, low).astype(BF)


def inner_kernel(info, x_ref, coef_ref, emis_ref, det_ref, adv_ref, keep_ref, send_ref):
    block, _, width = x_ref.shape
    own_first = info[1] == 0

    def group(g, carry):
        at = pl.ds(pl.multiple_of(g * 16, 16), 16)
        step = stepper(coef_ref, 0, offsets(det_ref, at, info[2], width), width)
        v = {r: x_ref[at, r, :] for r in (0, 1)}
        first = {}
        prints = {}
        for r in range(1, 7):
            v[r + 1] = x_ref[at, r + 1, :]
            first[r] = step(r, v[r - 1], v[r], v[r + 1])
            if r >= 3:
                q = r - 1
                out = step(q, first[q - 1], first[q], first[q + 1])
                adv_ref[at, q, :] = out
                prints[q] = out * emis_ref[q:q + 1, :]
                if q >= 4:
                    put(keep_ref, send_ref, at, q - 4, own_first, prints[q - 2], prints[q])
        return carry

    lax.fori_loop(0, block // 16, group, 0)


def outer_kernel(info, x_ref, up_ref, down_ref, coef_ref, emis_ref, det_ref, mid_ref, adv_ref, keep_ref, send_ref):
    block, _, width = x_ref.shape
    own_first = info[1] == 0

    def group(g, carry):
        at = pl.ds(pl.multiple_of(g * 16, 16), 16)
        step = stepper(coef_ref, 1, offsets(det_ref, at, info[2], width), width)

        def value(r):
            if r < 0:
                return up_ref[r + 2, at, :].astype(jnp.float32)
            if r > 7:
                return down_ref[r - 8, at, :].astype(jnp.float32)
            return x_ref[at, r, :]

        prints = {}
        for base in (-1, 5):
            v = {r: value(r) for r in (base - 1, base)}
            first = {}
            for r in range(base, base + 4):
                v[r + 1] = value(r + 1)
                first[r] = step(r, v[r - 1], v[r], v[r + 1])
                if r >= base + 2:
                    q = r - 1
                    out = step(q, first[q - 1], first[q], first[q + 1])
                    adv_ref[at, q, :] = out
                    prints[q] = out * emis_ref[q:q + 1, :]
        for r in range(2, 6):
            adv_ref[at, r, :] = mid_ref[at, r, :]
        for p in range(2):
            put(keep_ref, send_ref, at, p, own_first, prints[p], prints[p + 6])
        return carry

    lax.fori_loop(0, block // 16, group, 0)


def stencil(kernel, info, field, halos, coef, emis, det, mid, work):
    groups, rows, width = field.shape
    block = 64
    count = groups // block
    half = count // 2
    cells = 2 * width

    def turned(i, info):
        return lax.rem(i + info[0] * half, count)

    fields = pl.BlockSpec((block, rows, width), lambda i, info: (turned(i, info), 0, 0))
    halo = pl.BlockSpec((2, block, width), lambda i, info: (0, turned(i, info), 0))
    prints = pl.BlockSpec((block, cells), lambda i, info: (i, 0))
    print_shape = jax.ShapeDtypeStruct((groups, cells), BF)
    operands = [field, *halos, coef, emis, det, *mid]
    return pl.pallas_call(
        kernel,
        grid_spec=pltpu.PrefetchScalarGridSpec(
            num_scalar_prefetch=1,
            grid=(count,),
            in_specs=[
                fields,
                *([halo] * len(halos)),
                pl.BlockSpec(coef.shape, lambda i, info: (0, 0, 0)),
                pl.BlockSpec((rows, width), lambda i, info: (0, 0)),
                pl.BlockSpec((block, 1), lambda i, info: (turned(i, info), 0)),
                *([fields] * len(mid)),
            ],
            out_specs=[fields, prints, prints],
        ),
        out_shape=[jax.ShapeDtypeStruct(field.shape, jnp.float32), print_shape, print_shape],
        input_output_aliases={len(operands): 0} if mid else {},
        cost_estimate=cost(work, 8 << 20),
        compiler_params=params(),
    )(info, *operands)


NT = (((1,), (1,)), ((), ()))


def dot(left, right):
    return lax.dot_general(left, right, NT, preferred_element_type=jnp.float32)


def gram_kernel(grows, info, *refs):
    out_ref = refs[-1]
    acc_ref = refs[-2] if grows else None
    own, nxt, last, last_s, mine, theirs = (refs[2 * k:2 * k + 2] for k in range(6))
    core, xl = info[0], info[1]
    rows, depth = own[0].shape
    half = depth // 2
    at = [pl.multiple_of(lax.rem(core + m, 2) * rows, rows) for m in range(2)]
    e, i = pl.program_id(0), pl.program_id(1)

    def put_block(a_ref, pair):
        for j in range(2):
            slot = lax.rem(j + xl, 2)
            first, second = pair(j, a_ref)
            for m, value in enumerate((first, second)):
                where = (0, 0, slot, slice(None), pl.ds(at[m], rows))
                out_ref[where] = (value if acc_ref is None else value + acc_ref[where])

    def here(j, a):
        return dot(a[...], own[j][...]), (
            dot(a[:, :half], mine[j][rows:, :]) + dot(a[:, half:], theirs[j][:rows, :])
        )

    def far(j, a):
        return dot(a[...], last[j][...]), (
            dot(a[:, :half], last_s[j][:, half:]) + dot(a[:, half:], last_s[j][:, :half])
        )

    for step, (lefts, pair) in enumerate(((own, here), (nxt, here), (nxt, far), (last, here))):
        for owner in range(2):
            @pl.when((e == step) & (i == owner))
            def _():
                put_block(lefts[owner], pair)


def partial_gram(info, operands, acc):
    rows = operands[0].shape[0]
    cols = 2 * rows
    whole = pl.BlockSpec(memory_space=pltpu.VMEM)
    block = pl.BlockSpec(
        (1, 1, 2, rows, cols),
        lambda e, i, info: (lax.rem(info[3] + e, 4), lax.rem(i + info[1], 2), 0, 0, 0),
    )
    return pl.pallas_call(
        lambda *refs: gram_kernel(bool(acc), *refs),
        grid_spec=pltpu.PrefetchScalarGridSpec(
            num_scalar_prefetch=1,
            grid=(4, 2),
            in_specs=[whole] * len(operands) + [block] * len(acc),
            out_specs=block,
        ),
        out_shape=jax.ShapeDtypeStruct((4, 2, 2, rows, cols), jnp.float32),
        cost_estimate=cost(16 * 2 * rows * cols * operands[0].shape[1], 20 << 20),
        compiler_params=params(),
    )(info, *operands, *acc)


def spread(keep, send):
    part = keep.shape[0] // 2
    result = []
    for mine in (keep, lax.ppermute(send, "xl", SWAP)):
        theirs = lax.ppermute(mine, "core", SWAP)
        own = jnp.concatenate([mine[:part], theirs[part:]], axis=1)
        nxt = lax.ppermute(own, "y", [((i + 1) % 4, i) for i in range(4)])
        last = lax.ppermute(own, "y", [(i, (i + 1) % 4) for i in range(4)])
        last_s = lax.ppermute(last, "core", SWAP)
        result.append((own, nxt, last, last_s, mine, theirs))
    return [array for pair in zip(*result) for array in pair]


def body(adjoint, courant, detector, sources, emission):
    groups, rows, width = adjoint.shape
    core = lax.axis_index("core")
    xl = lax.axis_index("xl")
    y = lax.axis_index("y")
    z = lax.axis_index("z")
    tile = lax.axis_index(GRID)
    first_cell = tile * rows * width
    info = jnp.stack([core, xl, first_cell, y]).astype(jnp.int32)
    count = lax.axis_size(GRID)
    forward = [(i, i + 1) for i in range(count - 1)]
    backward = [(i + 1, i) for i in range(count - 1)]

    top, bottom = edges(adjoint)
    up = lax.ppermute(bottom, GRID, forward)
    down = lax.ppermute(top, GRID, backward)
    coef_up = lax.ppermute(courant[:, rows - 1:], GRID, forward)
    coef_down = lax.ppermute(courant[:, :1], GRID, backward)
    columns = jnp.arange(width)

    def weights(c):
        return jnp.stack([
            c[0],
            c[1],
            jnp.where(columns == width - 1, 0.0, c[2]),
            jnp.where(columns == 0, 0.0, c[3]),
            1.0 - (c[0] + c[1] + c[2] + c[3]),
        ])

    local = sources - first_cell
    by_row = jnp.where(
        (local // width)[None, :] == jnp.arange(rows)[:, None], emission[None, :], 0.0
    )
    by_col = ((local % width)[:, None] == columns[None, :]).astype(jnp.float32)
    emis = jnp.dot(by_row, by_col, precision=lax.Precision.HIGHEST)
    det = detector[:, None]

    mid, keep, send = stencil(
        inner_kernel, info, adjoint, [], weights(courant), emis, det, [], 8 << 20
    )
    parts = spread(keep, send)
    total = partial_gram(info, parts, [])

    extended = jnp.concatenate([coef_up, courant, coef_down], axis=1)
    field, keep, send = stencil(
        outer_kernel, info, adjoint, [up, down], weights(extended), emis, det, [mid], 8 << 20
    )
    parts = spread(keep, send)
    total = partial_gram(info, parts, [total])

    half = jnp.float16
    packed = (total * LIFT).astype(half).reshape(16, groups // 2, groups)
    pieces = lax.all_to_all(packed, PLANE, 0, 0, tiled=True)
    summed = jnp.sum(pieces.astype(jnp.float32), axis=0)
    moves = [((i + 2) % 4 * 4 + i, (i + 1) % 4 * 4 + (i + 3) % 4) for i in range(4)]
    moved = lax.ppermute((summed * (1.0 / 16)).astype(half), ("z", "y"), moves)
    moved = moved.astype(jnp.float32) * 16.0
    summed = jnp.where(lax.rem(y + 2, 4) == z, moved, summed)
    total_sources = sources.shape[0] * count
    return field, summed * jnp.float32(1.0 / (LIFT * total_sources))


def solution(mesh):
    fine = Mesh(mesh.devices.reshape(4, 2, 2, 4, 2), ("z", "xh", "core", "y", "xl"))
    rec = ("y", "xl")
    in_specs = (P(rec, GRID, None), P(None, GRID, None), P(rec), P(GRID), P(GRID))
    out_specs = (P(rec, GRID, None), P(GRID, rec))
    return jax.shard_map(body, mesh=fine, in_specs=in_specs, out_specs=out_specs, check_vma=False)
```

```python
import jax
import jax.numpy as jnp
from jax import lax
from jax.experimental import pallas as pl
from jax.experimental.pallas import tpu as pltpu
from jax.sharding import Mesh, PartitionSpec as P

GRID = ("z", "xh", "core")
XS = ("xh", "xl")
HALF = jnp.float16
BF = jnp.bfloat16
VMEM_LIMIT = 16 * 1024 * 1024
LIFT = 1.0 / 256
SWAP = [(0, 1), (1, 0)]
INNER = 100 << 20
OUTER = 20 << 20


def params():
    return pltpu.CompilerParams(vmem_limit_bytes=VMEM_LIMIT)


def cost(flops, moved):
    return pl.CostEstimate(flops=flops, bytes_accessed=moved, transcendentals=0)


def edge_kernel(x_ref, top_ref, bot_ref):
    top_ref[0] = x_ref[:, 0, :].astype(BF)
    top_ref[1] = x_ref[:, 1, :].astype(BF)
    bot_ref[0] = x_ref[:, 6, :].astype(BF)
    bot_ref[1] = x_ref[:, 7, :].astype(BF)


def edges(field):
    groups, rows, width = field.shape
    block = 64
    shape = jax.ShapeDtypeStruct((2, groups, width), BF)
    spec = pl.BlockSpec((2, block, width), lambda i: (0, i, 0))
    return pl.pallas_call(
        edge_kernel,
        grid=(groups // block,),
        in_specs=[pl.BlockSpec((block, rows, width), lambda i: (i, 0, 0))],
        out_specs=[spec, spec],
        out_shape=[shape, shape],
        cost_estimate=cost(1000, 6 << 20),
        compiler_params=params(),
    )(field)


def stepper(coef_ref, offset, delta, width):
    def step(r, south, center, north):
        east = pltpu.roll(center, width - 1, 1)
        west = pltpu.roll(center, 1, 1)
        at = r + offset
        c = [coef_ref[k, at:at + 1, :] for k in range(5)]
        pulse = jnp.where(delta == r * width, 1.0, 0.0)
        return c[4] * center + c[0] * north + c[1] * south + c[2] * east + c[3] * west + pulse

    return step


def offsets(det_ref, at, first_cell, width):
    return det_ref[at, :] - first_cell - lax.broadcasted_iota(jnp.int32, (16, width), 1)


def put(keep_ref, send_ref, at, p, own_first, low, high):
    width = low.shape[1]
    cols = pl.ds(p * width, width)
    keep_ref[at, cols] = jnp.where(own_first, low, high).astype(BF)
    send_ref[at, cols] = jnp.where(own_first, high, low).astype(BF)


def inner_kernel(info, x_ref, coef_ref, emis_ref, det_ref, adv_ref, keep_ref, send_ref):
    block, _, width = x_ref.shape
    own_first = info[1] == 0

    def group(g, carry):
        at = pl.ds(pl.multiple_of(g * 16, 16), 16)
        step = stepper(coef_ref, 0, offsets(det_ref, at, info[2], width), width)
        v = {r: x_ref[at, r, :] for r in (0, 1)}
        first = {}
        prints = {}
        for r in range(1, 7):
            v[r + 1] = x_ref[at, r + 1, :]
            first[r] = step(r, v[r - 1], v[r], v[r + 1])
            if r >= 3:
                q = r - 1
                out = step(q, first[q - 1], first[q], first[q + 1])
                adv_ref[at, q, :] = out
                prints[q] = out * emis_ref[q:q + 1, :]
                if q >= 4:
                    put(keep_ref, send_ref, at, q - 4, own_first, prints[q - 2], prints[q])
        return carry

    lax.fori_loop(0, block // 16, group, 0, unroll=2)


def outer_kernel(info, x_ref, up_ref, down_ref, coef_ref, emis_ref, det_ref, mid_ref, adv_ref, keep_ref, send_ref):
    block, _, width = x_ref.shape
    own_first = info[1] == 0

    def group(g, carry):
        at = pl.ds(pl.multiple_of(g * 16, 16), 16)
        step = stepper(coef_ref, 1, offsets(det_ref, at, info[2], width), width)

        def value(r):
            if r < 0:
                return up_ref[r + 2, at, :].astype(jnp.float32)
            if r > 7:
                return down_ref[r - 8, at, :].astype(jnp.float32)
            return x_ref[at, r, :]

        prints = {}
        for base in (-1, 5):
            v = {r: value(r) for r in (base - 1, base)}
            first = {}
            for r in range(base, base + 4):
                v[r + 1] = value(r + 1)
                first[r] = step(r, v[r - 1], v[r], v[r + 1])
                if r >= base + 2:
                    q = r - 1
                    out = step(q, first[q - 1], first[q], first[q + 1])
                    adv_ref[at, q, :] = out
                    prints[q] = out * emis_ref[q:q + 1, :]
        for r in range(2, 6):
            adv_ref[at, r, :] = mid_ref[at, r, :]
        for p in range(2):
            put(keep_ref, send_ref, at, p, own_first, prints[p], prints[p + 6])
        return carry

    lax.fori_loop(0, block // 16, group, 0, unroll=2)


def stencil(kernel, info, field, halos, coef, emis, det, mid, work):
    groups, rows, width = field.shape
    block = 64
    count = groups // block
    half = count // 2
    cells = 2 * width

    def turned(i, info):
        return lax.rem(i + info[0] * half, count)

    fields = pl.BlockSpec((block, rows, width), lambda i, info: (turned(i, info), 0, 0))
    halo = pl.BlockSpec((2, block, width), lambda i, info: (0, turned(i, info), 0))
    prints = pl.BlockSpec((block, cells), lambda i, info: (i, 0))
    print_shape = jax.ShapeDtypeStruct((groups, cells), BF)
    operands = [field, *halos, coef, emis, det, *mid]
    return pl.pallas_call(
        kernel,
        grid_spec=pltpu.PrefetchScalarGridSpec(
            num_scalar_prefetch=1,
            grid=(count,),
            in_specs=[
                fields,
                *([halo] * len(halos)),
                pl.BlockSpec(coef.shape, lambda i, info: (0, 0, 0)),
                pl.BlockSpec((rows, width), lambda i, info: (0, 0)),
                pl.BlockSpec((block, 1), lambda i, info: (turned(i, info), 0)),
                *([fields] * len(mid)),
            ],
            out_specs=[fields, prints, prints],
        ),
        out_shape=[jax.ShapeDtypeStruct(field.shape, jnp.float32), print_shape, print_shape],
        input_output_aliases={len(operands): 0} if mid else {},
        cost_estimate=cost(1000, work),
        compiler_params=params(),
    )(info, *operands)


NT = (((1,), (1,)), ((), ()))


def dot(left, right):
    return lax.dot_general(left, right, NT, preferred_element_type=jnp.float32)


def gram_kernel(grows, info, *refs):
    stack, outs = refs[-1], refs[-3:-1]
    accs = refs[12:14] if grows else None
    own, own_s, nxt, nxt_s, last, last_s = (refs[2 * k:2 * k + 2] for k in range(6))
    core, xl, y, xpos = info[0], info[1], info[3], info[4]
    rows = nxt_s[0].shape[0]
    half = own[0].shape[1]
    part = rows // 2
    lefts = []
    for e, tile, sibling, first in ((1, nxt, nxt_s, 0), (0, own, own_s, rows), (3, last, last_s, rows)):
        for i in range(2):
            at = pl.ds(len(lefts) * rows, rows)
            stack[at, :half] = tile[i][:rows, :]
            stack[at, half:] = sibling[i][first:first + rows, :]
            lefts.append((e, i))

    for j in range(2):
        for m in range(2):
            mine = slice(m * rows, (m + 1) * rows)
            theirs = slice((1 - m) * rows, (2 - m) * rows)
            here = dot(stack[:, :half], own[j][mine, :]) + dot(stack[:, half:], own_s[j][theirs, :])
            far = dot(stack[:2 * rows, :half], last[j][mine, :]) + dot(
                stack[:2 * rows, half:], last_s[j][theirs, :]
            )
            cols = pl.ds(pl.multiple_of(lax.rem(core + m, 2) * rows, rows), rows)
            values = [(e, i, here[k * rows:(k + 1) * rows]) for k, (e, i) in enumerate(lefts)]
            values += [(2, i, far[i * rows:(i + 1) * rows]) for i in range(2)]
            for e, i, value in values:
                at_z = lax.rem(y + e, 4)
                at_x = lax.rem(lax.rem(i + xl, 2) * 2 + lax.rem(j + xl, 2) + 4 - xpos, 4)
                for upper, slot in enumerate((at_z * 4 + at_x, at_x * 4 + at_z)):
                    piece = value[upper * part:(upper + 1) * part]
                    if accs is not None:
                        piece = piece + accs[upper][slot, :, cols]
                    outs[upper][slot, :, cols] = piece


def partial_gram(info, operands, acc):
    rows, half = operands[0].shape
    rows = rows // 2
    whole = pl.BlockSpec(memory_space=pltpu.VMEM)
    shape = jax.ShapeDtypeStruct((16, rows // 2, 2 * rows), jnp.float32)
    return pl.pallas_call(
        lambda *refs: gram_kernel(bool(acc), *refs),
        in_specs=[pl.BlockSpec(memory_space=pltpu.SMEM)] + [whole] * (len(operands) + len(acc)),
        out_specs=[whole, whole],
        out_shape=[shape, shape],
        scratch_shapes=[pltpu.VMEM((6 * rows, 2 * half), BF)],
        cost_estimate=cost(1000, 8 << 20),
        compiler_params=params(),
    )(info, *operands, *acc)


def to_four(pieces, axis):
    total = pieces[0].astype(jnp.float32)
    for d in (1, 2, 3):
        came = lax.ppermute(pieces[d], axis, [(i, (i + d) % 4) for i in range(4)])
        total = total + came.astype(jnp.float32)
    return total * 0.25


def after(value, *others):
    return lax.optimization_barrier((value, others))[0]


def along_y(own):
    nxt = lax.ppermute(own, "y", [((i + 1) % 4, i) for i in range(4)])
    last = lax.ppermute(own, "y", [(i, (i + 1) % 4) for i in range(4)])
    return nxt, last


def siblings(own, nxt, last):
    part = own.shape[0] // 2
    own_s = lax.ppermute(own, "core", SWAP)
    nxt_s = lax.ppermute(nxt[part:], "core", SWAP)
    last_s = lax.ppermute(last, "core", SWAP)
    return own, own_s, nxt, nxt_s, last, last_s


def gram_operands(keep, keep_y, other, other_y):
    return [
        array for pair in zip(siblings(keep, *keep_y), siblings(other, *other_y)) for array in pair
    ]


def mean_of_four(pieces):
    return jnp.sum(pieces.astype(jnp.float32), axis=0) * 0.25


def body(adjoint, courant, detector, sources, emission):
    groups, rows, width = adjoint.shape
    core = lax.axis_index("core")
    xl = lax.axis_index("xl")
    y = lax.axis_index("y")
    z = lax.axis_index("z")
    tile = lax.axis_index(GRID)
    first_cell = tile * rows * width
    xpos = lax.axis_index(XS)
    info = jnp.stack([core, xl, first_cell, y, xpos]).astype(jnp.int32)
    count = lax.axis_size(GRID)
    forward = [(i, i + 1) for i in range(count - 1)]
    backward = [(i + 1, i) for i in range(count - 1)]

    top, bottom = edges(adjoint)
    up = lax.ppermute(bottom, GRID, forward)
    down = lax.ppermute(top, GRID, backward)
    near = after(courant, top)
    coef_up = lax.ppermute(near[:, rows - 1:], GRID, forward)
    coef_down = lax.ppermute(near[:, :1], GRID, backward)
    columns = jnp.arange(width)

    def weights(c):
        return jnp.stack([
            c[0],
            c[1],
            jnp.where(columns == width - 1, 0.0, c[2]),
            jnp.where(columns == 0, 0.0, c[3]),
            1.0 - (c[0] + c[1] + c[2] + c[3]),
        ])

    local = sources - first_cell
    by_row = jnp.where(
        (local // width)[None, :] == jnp.arange(rows)[:, None], emission[None, :], 0.0
    )
    by_col = ((local % width)[:, None] == columns[None, :]).astype(jnp.float32)
    emis = jnp.dot(by_row, by_col, precision=lax.Precision.HIGHEST)
    det = detector[:, None]

    weights_in = weights(courant)
    mid, keep, send = stencil(
        inner_kernel, after(info, top, bottom), adjoint, [], weights_in, emis, det, [], INNER
    )
    other = lax.ppermute(send, "xl", SWAP)
    keep_y = along_y(after(keep, up, down))
    other_y = along_y(after(other, keep_y))
    totals = partial_gram(info, gram_operands(keep, keep_y, other, other_y), [])

    extended = jnp.concatenate([coef_up, courant, coef_down], axis=1)
    field, keep, send = stencil(
        outer_kernel, after(info, keep_y), adjoint, [up, down], weights(extended), emis, det,
        [mid], OUTER
    )
    other = lax.ppermute(send, "xl", SWAP)
    keep_y = along_y(keep)
    other_y = along_y(after(other, keep_y, totals))
    totals = partial_gram(info, gram_operands(keep, keep_y, other, other_y), totals)

    along_z, along_x = [
        (total * LIFT).astype(HALF).reshape(4, 4, groups // 4, groups) for total in totals
    ]
    along_z = lax.all_to_all(along_z, "z", 0, 0, tiled=True)
    along_x = after(to_four(along_x, XS).astype(HALF), along_z)
    along_z = mean_of_four(along_z).astype(HALF)
    along_x = mean_of_four(lax.all_to_all(along_x, "z", 0, 0, tiled=True))
    along_z = to_four(along_z, XS)
    summed = jnp.concatenate([along_z, along_x], axis=0)
    moves = [((i + 2) % 4 * 4 + i, (i + 1) % 4 * 4 + (i + 3) % 4) for i in range(4)]
    moved = lax.ppermute(summed.astype(HALF), ("z", "y"), moves).astype(jnp.float32)
    summed = jnp.where(lax.rem(y + 2, 4) == z, moved, summed)
    total_sources = sources.shape[0] * count
    return field, summed * jnp.float32(16.0 / (LIFT * total_sources))


def solution(mesh):
    fine = Mesh(mesh.devices.reshape(4, 2, 2, 4, 2), ("z", "xh", "core", "y", "xl"))
    rec = ("y", "xl")
    in_specs = (P(rec, GRID, None), P(None, GRID, None), P(rec), P(GRID), P(GRID))
    out_specs = (P(rec, GRID, None), P(GRID, rec))
    return jax.shard_map(body, mesh=fine, in_specs=in_specs, out_specs=out_specs, check_vma=False)
```

```python
import jax
import jax.numpy as jnp
from jax import lax
from jax.experimental import pallas as pl
from jax.experimental.pallas import tpu as pltpu
from jax.sharding import Mesh, PartitionSpec as P

GRID = ("z", "xh", "core")
XS = ("xh", "xl")
HALF = jnp.float16
BF = jnp.bfloat16
VMEM_LIMIT = 16 * 1024 * 1024
ALMOST_ALL = 60 * 1024 * 1024
LIFT = 1.0 / 256
SWAP = [(0, 1), (1, 0)]
INNER = 100 << 20
OUTER = 20 << 20


def params():
    return pltpu.CompilerParams(vmem_limit_bytes=VMEM_LIMIT)


def cost(flops, moved):
    return pl.CostEstimate(flops=flops, bytes_accessed=moved, transcendentals=0)


def edge_kernel(x_ref, c_ref, top_ref, bot_ref):
    i = pl.program_id(0)
    block, rows, _ = x_ref.shape
    at = pl.ds(pl.multiple_of(i * block, block), block)
    for out_ref, first, edge in ((top_ref, 0, 0), (bot_ref, rows - 2, rows - 1)):
        out_ref[0, at, :] = x_ref[:, first, :].astype(BF)
        out_ref[1, at, :] = x_ref[:, first + 1, :].astype(BF)

        @pl.when(i == 0)
        def _():
            rest = c_ref[:, edge, :]
            terms = []
            for _ in range(3):
                terms.append(rest.astype(BF).astype(jnp.float32))
                rest = rest - terms[-1]
            packed = jnp.concatenate(terms + [jnp.zeros_like(rest)], axis=0).astype(BF)
            last = out_ref.shape[1] - packed.shape[0]
            for k in range(2):
                out_ref[k, last:, :] = packed


def edges(field, courant):
    groups, rows, width = field.shape
    block = 64
    shape = jax.ShapeDtypeStruct((2, groups + 16, width), BF)
    spec = pl.BlockSpec(shape.shape, lambda i: (0, 0, 0))
    return pl.pallas_call(
        edge_kernel,
        grid=(groups // block,),
        in_specs=[
            pl.BlockSpec((block, rows, width), lambda i: (i, 0, 0)),
            pl.BlockSpec(courant.shape, lambda i: (0, 0, 0)),
        ],
        out_specs=[spec, spec],
        out_shape=[shape, shape],
        cost_estimate=cost(1000, 6 << 20),
        compiler_params=pltpu.CompilerParams(vmem_limit_bytes=ALMOST_ALL),
    )(field, courant)


def edge_weights(halo, groups):
    return jnp.sum(halo[0, groups:groups + 12].astype(jnp.float32).reshape(3, 4, 1, -1), axis=0)


def stepper(coef_ref, offset, delta, width):
    def step(r, south, center, north):
        east = pltpu.roll(center, width - 1, 1)
        west = pltpu.roll(center, 1, 1)
        at = r + offset
        c = [coef_ref[k, at:at + 1, :] for k in range(5)]
        pulse = jnp.where(delta == r * width, 1.0, 0.0)
        return c[4] * center + c[0] * north + c[1] * south + c[2] * east + c[3] * west + pulse

    return step


def offsets(det_ref, at, first_cell, width):
    return det_ref[at, :] - first_cell - lax.broadcasted_iota(jnp.int32, (16, width), 1)


def put(keep_ref, send_ref, at, p, own_first, low, high):
    width = low.shape[1]
    cols = pl.ds(p * width, width)
    keep_ref[at, cols] = jnp.where(own_first, low, high).astype(BF)
    send_ref[at, cols] = jnp.where(own_first, high, low).astype(BF)


def inner_kernel(info, x_ref, coef_ref, emis_ref, det_ref, adv_ref, keep_ref, send_ref):
    block, _, width = x_ref.shape
    own_first = info[1] == 0

    def group(g, carry):
        at = pl.ds(pl.multiple_of(g * 16, 16), 16)
        step = stepper(coef_ref, 0, offsets(det_ref, at, info[2], width), width)
        v = {r: x_ref[at, r, :] for r in (0, 1)}
        first = {}
        prints = {}
        for r in range(1, 7):
            v[r + 1] = x_ref[at, r + 1, :]
            first[r] = step(r, v[r - 1], v[r], v[r + 1])
            if r >= 3:
                q = r - 1
                out = step(q, first[q - 1], first[q], first[q + 1])
                adv_ref[at, q, :] = out
                prints[q] = out * emis_ref[q:q + 1, :]
                if q >= 4:
                    put(keep_ref, send_ref, at, q - 4, own_first, prints[q - 2], prints[q])
        return carry

    lax.fori_loop(0, block // 16, group, 0, unroll=4)


def outer_kernel(info, x_ref, up_ref, down_ref, coef_ref, emis_ref, det_ref, mid_ref, adv_ref, keep_ref, send_ref):
    block, _, width = x_ref.shape
    own_first = info[1] == 0

    def group(g, carry):
        at = pl.ds(pl.multiple_of(g * 16, 16), 16)
        step = stepper(coef_ref, 1, offsets(det_ref, at, info[2], width), width)

        def value(r):
            if r < 0:
                return up_ref[r + 2, at, :].astype(jnp.float32)
            if r > 7:
                return down_ref[r - 8, at, :].astype(jnp.float32)
            return x_ref[at, r, :]

        prints = {}
        for base in (-1, 5):
            v = {r: value(r) for r in (base - 1, base)}
            first = {}
            for r in range(base, base + 4):
                v[r + 1] = value(r + 1)
                first[r] = step(r, v[r - 1], v[r], v[r + 1])
                if r >= base + 2:
                    q = r - 1
                    out = step(q, first[q - 1], first[q], first[q + 1])
                    adv_ref[at, q, :] = out
                    prints[q] = out * emis_ref[q:q + 1, :]
        for r in range(2, 6):
            adv_ref[at, r, :] = mid_ref[at, r, :]
        for p in range(2):
            put(keep_ref, send_ref, at, p, own_first, prints[p], prints[p + 6])
        return carry

    lax.fori_loop(0, block // 16, group, 0, unroll=4)


def stencil(kernel, info, field, halos, coef, emis, det, mid, work, limit):
    groups, rows, width = field.shape
    block = 64
    count = groups // block
    half = count // 2
    cells = 2 * width

    def turned(i, info):
        return lax.rem(i + info[0] * half, count)

    fields = pl.BlockSpec((block, rows, width), lambda i, info: (turned(i, info), 0, 0))
    halo = pl.BlockSpec((2, block, width), lambda i, info: (0, turned(i, info), 0))
    prints = pl.BlockSpec((block, cells), lambda i, info: (i, 0))
    print_shape = jax.ShapeDtypeStruct((groups, cells), BF)
    operands = [field, *halos, coef, emis, det, *mid]
    return pl.pallas_call(
        kernel,
        grid_spec=pltpu.PrefetchScalarGridSpec(
            num_scalar_prefetch=1,
            grid=(count,),
            in_specs=[
                fields,
                *([halo] * len(halos)),
                pl.BlockSpec(coef.shape, lambda i, info: (0, 0, 0)),
                pl.BlockSpec((rows, width), lambda i, info: (0, 0)),
                pl.BlockSpec((block, 1), lambda i, info: (turned(i, info), 0)),
                *([fields] * len(mid)),
            ],
            out_specs=[fields, prints, prints],
        ),
        out_shape=[jax.ShapeDtypeStruct(field.shape, jnp.float32), print_shape, print_shape],
        input_output_aliases={len(operands): 0} if mid else {},
        cost_estimate=cost(1000, work),
        compiler_params=pltpu.CompilerParams(vmem_limit_bytes=limit),
    )(info, *operands)


NT = (((1,), (1,)), ((), ()))


def dot(left, right):
    return lax.dot_general(left, right, NT, preferred_element_type=jnp.float32)


def gram_kernel(grows, info, *refs):
    if grows:
        accs, (*outs, done_ref, stack, acc_buf, sem) = refs[12:14], refs[15:]
        copies = [
            pltpu.make_async_copy(accs[upper], acc_buf.at[upper], sem.at[upper]) for upper in range(2)
        ]
    else:
        *outs, done_ref, stack = refs[12:]
    done_ref[...] = jnp.zeros_like(done_ref)
    own, own_s, nxt, nxt_s, last, last_s = (refs[2 * k:2 * k + 2] for k in range(6))
    core, xl, y, xpos, z = info[0], info[1], info[3], info[4], info[5]
    rows = nxt_s[0].shape[0]
    half = own[0].shape[1]
    part = rows // 2
    m = pl.program_id(0)
    places = [(e, i) for e in (1, 0, 3) for i in range(2)]

    @pl.when(m == 0)
    def _():
        if grows:
            for copy in copies:
                copy.start()
        for k, (e, i) in enumerate(places):
            tile, sibling, first = ((own, own_s, rows), (nxt, nxt_s, 0), None, (last, last_s, rows))[e]
            at = pl.ds(k * rows, rows)
            stack[at, :half] = tile[i][:rows, :]
            stack[at, half:] = sibling[i][first:first + rows, :]

    mine = pl.ds(pl.multiple_of(m * rows, rows), rows)
    theirs = pl.ds(pl.multiple_of((1 - m) * rows, rows), rows)
    cols = slice(None)
    if grows:
        cols = pl.ds(pl.multiple_of(lax.rem(core + m, 2) * rows, rows), rows)
    for j in range(2):
        here = dot(stack[:, :half], own[j][mine, :]) + dot(stack[:, half:], own_s[j][theirs, :])
        far = dot(stack[:2 * rows, :half], last[j][mine, :]) + dot(
            stack[:2 * rows, half:], last_s[j][theirs, :]
        )
        if grows and j == 0:
            @pl.when(m == 0)
            def _():
                for copy in copies:
                    copy.wait()
        values = [(e, i, here[k * rows:(k + 1) * rows]) for k, (e, i) in enumerate(places)]
        values += [(2, i, far[i * rows:(i + 1) * rows]) for i in range(2)]
        for e, i, value in values:
            at_z = lax.rem(y + e + 4 - z, 4)
            at_x = lax.rem(lax.rem(i + xl, 2) * 2 + lax.rem(j + xl, 2) + 4 - xpos, 4)
            for upper, slot in enumerate((at_z * 4 + at_x, at_x * 4 + at_z)):
                piece = value[upper * part:(upper + 1) * part]
                if grows:
                    piece = piece + acc_buf[upper, slot, :, cols]
                outs[upper][slot, :, cols] = piece


def partial_gram(info, operands, acc):
    rows, half = operands[0].shape
    rows = rows // 2
    whole = pl.BlockSpec(memory_space=pltpu.VMEM)
    shape = (jax.ShapeDtypeStruct if acc else pltpu.HBM)((16, rows // 2, 2 * rows), jnp.float32)
    block = pl.BlockSpec(
        (16, rows // 2, rows), lambda m, info: (0, 0, lax.rem(info[0] + m, 2))
    )
    far = pl.BlockSpec(memory_space=pltpu.HBM)
    grown = [
        pltpu.VMEM((2, 16, rows // 2, 2 * rows), jnp.float32), pltpu.SemaphoreType.DMA((2,))
    ]
    token = pl.BlockSpec((8, 128), lambda m, info: (0, 0))
    return pl.pallas_call(
        lambda *refs: gram_kernel(bool(acc), *refs),
        grid_spec=pltpu.PrefetchScalarGridSpec(
            num_scalar_prefetch=1,
            grid=(2,),
            in_specs=[whole] * len(operands) + [far, far, token][:len(acc)],
            out_specs=([whole, whole] if acc else [block, block])
            + [token],
            scratch_shapes=[pltpu.VMEM((6 * rows, 2 * half), BF)] + (grown if acc else []),
        ),
        out_shape=[shape, shape, jax.ShapeDtypeStruct((8, 128), jnp.float32)],
        cost_estimate=cost(1000, 8 << 20),
        compiler_params=pltpu.CompilerParams(vmem_limit_bytes=(46 if acc else 24) << 20),
    )(info, *operands, *acc)


def place(z, y, x):
    return ((z % 4 * 2 + x % 4 // 2) * 4 + y % 4) * 2 + x % 2


def to_place(pieces, dz, dx):
    z, y = lax.axis_index("z"), lax.axis_index("y")
    total = 0.0
    for d in range(4):
        pairs = []
        for zi in range(4):
            for yi in range(4):
                for xi in range(4):
                    zt, yt, xt = zi + d * dz, yi, xi + d * dx
                    if (zt - yt) % 4 == 2:
                        zt, yt = zt - 1, yt - 1
                    elif d == 0:
                        continue
                    pairs.append((place(zi, yi, xi), place(zt, yt, xt)))
        came = lax.ppermute(pieces[d], ("z", "xh", "y", "xl"), pairs)
        if d == 0:
            came = jnp.where(lax.rem(y + 2, 4) == z, came, pieces[0])
        total = total + came.astype(jnp.float32)
    return total * 0.25


def to_four(pieces, axis):
    total = pieces[0].astype(jnp.float32)
    for d in (1, 2, 3):
        came = lax.ppermute(pieces[d], axis, [(i, (i + d) % 4) for i in range(4)])
        total = total + came.astype(jnp.float32)
    return total * 0.25


def after(value, *others):
    return lax.optimization_barrier((value, others))[0]


def along_y(own):
    nxt = lax.ppermute(own, "y", [((i + 1) % 4, i) for i in range(4)])
    last = lax.ppermute(own, "y", [(i, (i + 1) % 4) for i in range(4)])
    return nxt, last


def siblings(own, nxt, last):
    part = own.shape[0] // 2
    own_s = lax.ppermute(own, "core", SWAP)
    nxt_s = lax.ppermute(nxt[part:], "core", SWAP)
    last_s = lax.ppermute(last, "core", SWAP)
    return own, own_s, nxt, nxt_s, last, last_s


def gram_operands(keep, keep_y, other, other_y):
    return [
        array for pair in zip(siblings(keep, *keep_y), siblings(other, *other_y)) for array in pair
    ]


def body(adjoint, courant, detector, sources, emission):
    groups, rows, width = adjoint.shape
    core = lax.axis_index("core")
    xl = lax.axis_index("xl")
    y = lax.axis_index("y")
    z = lax.axis_index("z")
    tile = lax.axis_index(GRID)
    first_cell = tile * rows * width
    xpos = lax.axis_index(XS)
    info = jnp.stack([core, xl, first_cell, y, xpos, z]).astype(jnp.int32)
    count = lax.axis_size(GRID)
    forward = [(i, i + 1) for i in range(count - 1)]
    backward = [(i + 1, i) for i in range(count - 1)]

    top, bottom = edges(adjoint, courant)
    up = lax.ppermute(bottom, GRID, forward)
    down = lax.ppermute(top, GRID, backward)
    columns = jnp.arange(width)

    def weights(c):
        return jnp.stack([
            c[0],
            c[1],
            jnp.where(columns == width - 1, 0.0, c[2]),
            jnp.where(columns == 0, 0.0, c[3]),
            1.0 - (c[0] + c[1] + c[2] + c[3]),
        ])

    local = sources - first_cell
    by_row = jnp.where(
        (local // width)[None, :] == jnp.arange(rows)[:, None], emission[None, :], 0.0
    )
    by_col = ((local % width)[:, None] == columns[None, :]).astype(jnp.float32)
    emis = jnp.dot(by_row, by_col, precision=lax.Precision.HIGHEST)
    det = detector[:, None]

    weights_in = weights(courant)
    mid, keep, send = stencil(
        inner_kernel, after(info, top, bottom), adjoint, [], weights_in, emis, det, [], INNER,
        VMEM_LIMIT,
    )
    other = lax.ppermute(send, "xl", SWAP)
    keep_y = along_y(after(keep, up, down))
    other_y = along_y(after(other, keep_y))
    *totals, done = partial_gram(info, gram_operands(keep, keep_y, other, other_y), [])

    extended = jnp.concatenate(
        [edge_weights(up, groups), courant, edge_weights(down, groups)], axis=1
    )
    field, keep, send = stencil(
        outer_kernel, after(info, keep_y), adjoint, [up, down], weights(extended), emis, det,
        [mid], OUTER, VMEM_LIMIT
    )
    other = lax.ppermute(send, "xl", SWAP)
    keep_y = along_y(keep)
    sent, done, _ = lax.optimization_barrier((other, done, keep_y))
    other_y = along_y(sent)
    *totals, _ = partial_gram(info, gram_operands(keep, keep_y, other, other_y), totals + [done])

    def packed(total):
        return (total * LIFT).astype(HALF).reshape(4, 4, groups // 4, groups)

    along_z = to_four(packed(totals[0]), "z").astype(HALF)
    along_x = to_four(packed(totals[1]), XS).astype(HALF)
    summed = jnp.concatenate([to_place(along_z, 0, 1), to_place(along_x, 1, 0)], axis=0)
    total_sources = sources.shape[0] * count
    return field, summed * jnp.float32(16.0 / (LIFT * total_sources))


def solution(mesh):
    fine = Mesh(mesh.devices.reshape(4, 2, 2, 4, 2), ("z", "xh", "core", "y", "xl"))
    rec = ("y", "xl")
    in_specs = (P(rec, GRID, None), P(None, GRID, None), P(rec), P(GRID), P(GRID))
    out_specs = (P(rec, GRID, None), P(GRID, rec))
    return jax.shard_map(body, mesh=fine, in_specs=in_specs, out_specs=out_specs, check_vma=False)
```

```python
import jax
import jax.numpy as jnp
from jax import lax
from jax.experimental import pallas as pl
from jax.experimental.pallas import tpu as pltpu
from jax.sharding import Mesh, PartitionSpec as P

GRID = ("z", "xh", "core")
XS = ("xh", "xl")
HALF = jnp.float16
BF = jnp.bfloat16
VMEM_LIMIT = 16 * 1024 * 1024
LIFT = 1.0 / 256
SWAP = [(0, 1), (1, 0)]
INNER = 100 << 20
OUTER = 20 << 20


def params():
    return pltpu.CompilerParams(vmem_limit_bytes=VMEM_LIMIT)


def cost(flops, moved):
    return pl.CostEstimate(flops=flops, bytes_accessed=moved, transcendentals=0)


def edge_kernel(x_ref, c_ref, top_ref, bot_ref):
    i = pl.program_id(0)
    block, rows, _ = x_ref.shape
    at = pl.ds(pl.multiple_of(i * block, block), block)
    for out_ref, first, edge in ((top_ref, 0, 0), (bot_ref, rows - 2, rows - 1)):
        out_ref[0, at, :] = x_ref[:, first, :].astype(BF)
        out_ref[1, at, :] = x_ref[:, first + 1, :].astype(BF)

        @pl.when(i == 0)
        def _():
            rest = c_ref[:, edge, :]
            terms = []
            for _ in range(3):
                terms.append(rest.astype(BF).astype(jnp.float32))
                rest = rest - terms[-1]
            packed = jnp.concatenate(terms + [jnp.zeros_like(rest)], axis=0).astype(BF)
            last = out_ref.shape[1] - packed.shape[0]
            for k in range(2):
                out_ref[k, last:, :] = packed


def edges(field, courant):
    groups, rows, width = field.shape
    block = 64
    shape = jax.ShapeDtypeStruct((2, groups + 16, width), BF)
    spec = pl.BlockSpec(shape.shape, lambda i: (0, 0, 0))
    return pl.pallas_call(
        edge_kernel,
        grid=(groups // block,),
        in_specs=[
            pl.BlockSpec((block, rows, width), lambda i: (i, 0, 0)),
            pl.BlockSpec(courant.shape, lambda i: (0, 0, 0)),
        ],
        out_specs=[spec, spec],
        out_shape=[shape, shape],
        cost_estimate=cost(1000, 6 << 20),
        compiler_params=params(),
    )(field, courant)


def edge_weights(halo, groups):
    return jnp.sum(halo[0, groups:groups + 12].astype(jnp.float32).reshape(3, 4, 1, -1), axis=0)


def stepper(coef_ref, offset, delta, width):
    def step(r, south, center, north):
        east = pltpu.roll(center, width - 1, 1)
        west = pltpu.roll(center, 1, 1)
        at = r + offset
        c = [coef_ref[k, at:at + 1, :] for k in range(5)]
        pulse = jnp.where(delta == r * width, 1.0, 0.0)
        return c[4] * center + c[0] * north + c[1] * south + c[2] * east + c[3] * west + pulse

    return step


def offsets(det_ref, at, first_cell, width):
    return det_ref[at, :] - first_cell - lax.broadcasted_iota(jnp.int32, (16, width), 1)


def put(keep_ref, send_ref, at, p, own_first, low, high):
    width = low.shape[1]
    cols = pl.ds(p * width, width)
    keep_ref[at, cols] = jnp.where(own_first, low, high).astype(BF)
    send_ref[at, cols] = jnp.where(own_first, high, low).astype(BF)


def inner_kernel(info, x_ref, coef_ref, emis_ref, det_ref, adv_ref, keep_ref, send_ref):
    block, rows, width = x_ref.shape
    own_first = info[1] == 0

    def group(g, carry):
        at = pl.ds(pl.multiple_of(g * 16, 16), 16)
        step = stepper(coef_ref, 0, offsets(det_ref, at, info[2], width), width)
        v = jnp.swapaxes(x_ref[at], 0, 1)
        first = {r: step(r, v[r - 1], v[r], v[r + 1]) for r in range(1, rows - 1)}
        out = {r: step(r, first[r - 1], first[r], first[r + 1]) for r in range(2, rows - 2)}
        tile = jnp.stack([out[min(max(r, 2), rows - 3)] for r in range(rows)])
        adv_ref[at] = jnp.swapaxes(tile, 0, 1)
        prints = {r: out[r] * emis_ref[r:r + 1, :] for r in out}
        for p in range(2):
            put(keep_ref, send_ref, at, p, own_first, prints[p + 2], prints[p + 4])
        return carry

    lax.fori_loop(0, block // 16, group, 0, unroll=2)


def outer_kernel(info, x_ref, up_ref, down_ref, coef_ref, emis_ref, det_ref, mid_ref, adv_ref, keep_ref, send_ref):
    block, rows, width = x_ref.shape
    own_first = info[1] == 0

    def group(g, carry):
        at = pl.ds(pl.multiple_of(g * 16, 16), 16)
        step = stepper(coef_ref, 1, offsets(det_ref, at, info[2], width), width)
        tile = jnp.swapaxes(x_ref[at], 0, 1)
        v = {r: tile[r] for r in range(rows)}
        for r in range(2):
            v[r - 2] = up_ref[r, at, :].astype(jnp.float32)
            v[r + rows] = down_ref[r, at, :].astype(jnp.float32)
        first = {r: step(r, v[r - 1], v[r], v[r + 1]) for r in (-1, 0, 1, 2, 5, 6, 7, 8)}
        out = {r: step(r, first[r - 1], first[r], first[r + 1]) for r in (0, 1, 6, 7)}
        tile = jnp.stack([out[r if r in out else (1 if r < 4 else 6)] for r in range(rows)])
        tile = jnp.swapaxes(tile, 0, 1)
        row = lax.broadcasted_iota(jnp.int32, tile.shape, 1)
        adv_ref[at] = jnp.where((row >= 2) & (row < 6), mid_ref[at], tile)
        prints = {r: out[r] * emis_ref[r:r + 1, :] for r in out}
        for p in range(2):
            put(keep_ref, send_ref, at, p, own_first, prints[p], prints[p + 6])
        return carry

    lax.fori_loop(0, block // 16, group, 0, unroll=2)


def stencil(kernel, info, field, halos, coef, emis, det, mid, work):
    groups, rows, width = field.shape
    block = 64
    count = groups // block
    half = count // 2
    cells = 2 * width

    def turned(i, info):
        return lax.rem(i + info[0] * half, count)

    fields = pl.BlockSpec((block, rows, width), lambda i, info: (turned(i, info), 0, 0))
    halo = pl.BlockSpec((2, block, width), lambda i, info: (0, turned(i, info), 0))
    prints = pl.BlockSpec((block, cells), lambda i, info: (i, 0))
    print_shape = jax.ShapeDtypeStruct((groups, cells), BF)
    operands = [field, *halos, coef, emis, det, *mid]
    return pl.pallas_call(
        kernel,
        grid_spec=pltpu.PrefetchScalarGridSpec(
            num_scalar_prefetch=1,
            grid=(count,),
            in_specs=[
                fields,
                *([halo] * len(halos)),
                pl.BlockSpec(coef.shape, lambda i, info: (0, 0, 0)),
                pl.BlockSpec((rows, width), lambda i, info: (0, 0)),
                pl.BlockSpec((block, 1), lambda i, info: (turned(i, info), 0)),
                *([fields] * len(mid)),
            ],
            out_specs=[fields, prints, prints],
        ),
        out_shape=[jax.ShapeDtypeStruct(field.shape, jnp.float32), print_shape, print_shape],
        input_output_aliases={len(operands): 0} if mid else {},
        cost_estimate=cost(1000, work),
        compiler_params=params(),
    )(info, *operands)


NT = (((1,), (1,)), ((), ()))


def dot(left, right):
    return lax.dot_general(left, right, NT, preferred_element_type=jnp.float32)


def gram_kernel(info, *refs):
    *refs, first_ref, second_ref, held, sem = refs
    outs = first_ref, second_ref
    own, own_s, nxt, nxt_s, last, last_s = (
        [(refs[2 * k + i], refs[2 * k + i + 12]) for i in range(2)] for k in range(6)
    )
    core, xl, y, xpos, z = info[0], info[1], info[3], info[4], info[5]
    rows = nxt_s[0][0].shape[0]
    half = own[0][0].shape[1]
    part = rows // 2
    sources = []
    for tile, sibling, start, start_s in (
        (nxt, nxt_s, 0, 0), (own, own_s, 0, rows), (last, last_s, 0, rows),
        (own, own_s, rows, 0), (last, last_s, rows, 0),
    ):
        sources += [(tile[i], sibling[i], start, start_s) for i in range(2)]
    copies = []
    for at, (tile, sibling, start, start_s) in enumerate(sources):
        for k in range(2):
            for side, (ref, first) in enumerate(((tile[k], start), (sibling[k], start_s))):
                copies.append(pltpu.make_async_copy(
                    ref.at[pl.ds(first, rows), :],
                    held.at[pl.ds(at * rows, rows), pl.ds((2 * k + side) * half, half)],
                    sem.at[len(copies)],
                ))
    for copy in copies:
        copy.start()
    for copy in copies:
        copy.wait()

    for j in range(2):
        for m in range(2):
            here, far = 2 + 4 * m + j, 4 + 4 * m + j
            here = dot(held[:6 * rows, :], held[here * rows:(here + 1) * rows, :])
            far = dot(held[:2 * rows, :], held[far * rows:(far + 1) * rows, :])
            cols = pl.ds(pl.multiple_of(lax.rem(core + m, 2) * rows, rows), rows)
            values = [(e, i, here[(2 * k + i) * rows:(2 * k + i + 1) * rows])
                      for k, e in enumerate((1, 0, 3)) for i in range(2)]
            values += [(2, i, far[i * rows:(i + 1) * rows]) for i in range(2)]
            for e, i, value in values:
                at_z = lax.rem(y + e + 4 - z, 4)
                at_x = lax.rem(lax.rem(i + xl, 2) * 2 + lax.rem(j + xl, 2) + 4 - xpos, 4)
                for upper, slot in enumerate((at_z * 4 + at_x, at_x * 4 + at_z)):
                    outs[upper][slot, :, cols] = value[upper * part:(upper + 1) * part]


def partial_gram(info, operands):
    rows, half = operands[0].shape
    rows = rows // 2
    whole = pl.BlockSpec(memory_space=pltpu.VMEM)
    shape = jax.ShapeDtypeStruct((16, rows // 2, 2 * rows), jnp.float32)
    return pl.pallas_call(
        gram_kernel,
        in_specs=[pl.BlockSpec(memory_space=pltpu.SMEM)]
        + [pl.BlockSpec(memory_space=pl.ANY)] * len(operands),
        out_specs=[whole, whole],
        out_shape=[shape, shape],
        scratch_shapes=[
            pltpu.VMEM((10 * rows, 4 * half), BF), pltpu.SemaphoreType.DMA((40,))
        ],
        cost_estimate=cost(1000, 8 << 20),
        compiler_params=pltpu.CompilerParams(vmem_limit_bytes=54 << 20),
    )(info, *operands)


def place(z, xh, y, xl):
    return ((z % 4 * 2 + xh) * 4 + y % 4) * 2 + xl


def home(z, y):
    return (z - 1, y - 1) if (z - y) % 4 == 2 else (z, y)


def to_homes(pieces, steps, axes=("z", "xh", "y", "xl")):
    total = 0.0
    stays = lax.rem(lax.axis_index("y") + 2, 4) != lax.axis_index("z")
    for d in range(steps):
        pairs = []
        for z in range(4):
            for y in range(4):
                target = home(z + d, y)
                if d or target != (z, y):
                    pairs += [
                        (place(z, xh, y, xl), place(target[0], xh, target[1], xl))
                        for xh in range(2) for xl in range(2)
                    ]
        came = lax.ppermute(pieces[d], axes, pairs)
        if d == 0:
            came = jnp.where(stays, pieces[0], came)
        total = total + came.astype(jnp.float32)
    return total


def to_four(pieces, axis):
    total = pieces[0].astype(jnp.float32)
    for d in (1, 2, 3):
        came = lax.ppermute(pieces[d], axis, [(i, (i + d) % 4) for i in range(4)])
        total = total + came.astype(jnp.float32)
    return total


def after(value, *others):
    return lax.optimization_barrier((value, others))[0]


def along_y(own):
    nxt = lax.ppermute(own, "y", [((i + 1) % 4, i) for i in range(4)])
    last = lax.ppermute(own, "y", [(i, (i + 1) % 4) for i in range(4)])
    return nxt, last


def siblings(own, nxt, last):
    part = own.shape[0] // 2
    own_s = lax.ppermute(own, "core", SWAP)
    nxt_s = lax.ppermute(nxt[part:], "core", SWAP)
    last_s = lax.ppermute(last, "core", SWAP)
    return own, own_s, nxt, nxt_s, last, last_s


def gram_operands(keep, keep_y, other, other_y):
    return [
        array for pair in zip(siblings(keep, *keep_y), siblings(other, *other_y)) for array in pair
    ]


def body(adjoint, courant, detector, sources, emission):
    groups, rows, width = adjoint.shape
    core = lax.axis_index("core")
    xl = lax.axis_index("xl")
    y = lax.axis_index("y")
    z = lax.axis_index("z")
    tile = lax.axis_index(GRID)
    first_cell = tile * rows * width
    xpos = lax.axis_index(XS)
    info = jnp.stack([core, xl, first_cell, y, xpos, z]).astype(jnp.int32)
    count = lax.axis_size(GRID)
    forward = [(i, i + 1) for i in range(count - 1)]
    backward = [(i + 1, i) for i in range(count - 1)]

    top, bottom = edges(adjoint, courant)
    up = lax.ppermute(bottom, GRID, forward)
    down = lax.ppermute(top, GRID, backward)
    columns = jnp.arange(width)

    def weights(c):
        return jnp.stack([
            c[0],
            c[1],
            jnp.where(columns == width - 1, 0.0, c[2]),
            jnp.where(columns == 0, 0.0, c[3]),
            1.0 - (c[0] + c[1] + c[2] + c[3]),
        ])

    local = sources - first_cell
    by_row = jnp.where(
        (local // width)[None, :] == jnp.arange(rows)[:, None], emission[None, :], 0.0
    )
    by_col = ((local % width)[:, None] == columns[None, :]).astype(jnp.float32)
    emis = jnp.dot(by_row, by_col, precision=lax.Precision.HIGHEST)
    det = detector[:, None]

    mid, keep, send = stencil(
        inner_kernel, after(info, top, bottom), adjoint, [], weights(courant), emis, det, [], INNER
    )
    other = lax.ppermute(send, "xl", SWAP)
    keep_y = along_y(after(keep, up, down))
    other_y = along_y(after(other, keep_y))
    operands = gram_operands(keep, keep_y, other, other_y)

    extended = jnp.concatenate(
        [edge_weights(up, groups), courant, edge_weights(down, groups)], axis=1
    )
    field, keep, send = stencil(
        outer_kernel, after(info, keep_y), adjoint, [up, down], weights(extended), emis, det,
        [mid], OUTER
    )
    other = lax.ppermute(send, "xl", SWAP)
    keep_y = along_y(after(keep, other_y))
    other_y = along_y(after(other, keep_y))
    operands += gram_operands(keep, keep_y, other, other_y)
    totals = partial_gram(info, operands)

    def packed(total):
        return (total * LIFT).astype(HALF).reshape(4, 4, groups // 4, groups)

    along_x, along_z = packed(totals[1]), packed(totals[0])
    along_x = (to_four(along_x, XS) * 0.25).astype(HALF)
    along_z = (to_homes(along_z, 4) * 0.25).astype(HALF)
    along_z = to_four(along_z, XS) * 0.25
    along_x = (to_four(along_x, "z") * 0.25).astype(HALF)
    summed = jnp.concatenate([along_z, to_homes(along_x[None], 1)], axis=0)
    total_sources = sources.shape[0] * count
    return field, summed * jnp.float32(16.0 / (LIFT * total_sources))


def solution(mesh):
    fine = Mesh(mesh.devices.reshape(4, 2, 2, 4, 2), ("z", "xh", "core", "y", "xl"))
    rec = ("y", "xl")
    in_specs = (P(rec, GRID, None), P(None, GRID, None), P(rec), P(GRID), P(GRID))
    out_specs = (P(rec, GRID, None), P(GRID, rec))
    return jax.shard_map(body, mesh=fine, in_specs=in_specs, out_specs=out_specs, check_vma=False)
```

```python
import jax
import jax.numpy as jnp
from jax import lax
from jax.experimental import pallas as pl
from jax.experimental.pallas import tpu as pltpu
from jax.sharding import Mesh, PartitionSpec as P

GRID = ("z", "xh", "core")
XS = ("xh", "xl")
HALF = jnp.float16
BF = jnp.bfloat16
VMEM_LIMIT = 16 * 1024 * 1024
LIFT = 1.0 / 256
SWAP = [(0, 1), (1, 0)]
INNER = 100 << 20
OUTER = 20 << 20


def params():
    return pltpu.CompilerParams(vmem_limit_bytes=VMEM_LIMIT)


def cost(flops, moved):
    return pl.CostEstimate(flops=flops, bytes_accessed=moved, transcendentals=0)


def edge_kernel(x_ref, c_ref, top_ref, bot_ref):
    i = pl.program_id(0)
    block, rows, _ = x_ref.shape
    at = pl.ds(pl.multiple_of(i * block, block), block)
    for out_ref, first, edge in ((top_ref, 0, 0), (bot_ref, rows - 2, rows - 1)):
        out_ref[0, at, :] = x_ref[:, first, :].astype(BF)
        out_ref[1, at, :] = x_ref[:, first + 1, :].astype(BF)

        @pl.when(i == 0)
        def _():
            rest = c_ref[:, edge, :]
            terms = []
            for _ in range(3):
                terms.append(rest.astype(BF).astype(jnp.float32))
                rest = rest - terms[-1]
            packed = jnp.concatenate(terms + [jnp.zeros_like(rest)], axis=0).astype(BF)
            last = out_ref.shape[1] - packed.shape[0]
            for k in range(2):
                out_ref[k, last:, :] = packed


def edges(field, courant):
    groups, rows, width = field.shape
    block = 64
    shape = jax.ShapeDtypeStruct((2, groups + 16, width), BF)
    spec = pl.BlockSpec(shape.shape, lambda i: (0, 0, 0))
    return pl.pallas_call(
        edge_kernel,
        grid=(groups // block,),
        in_specs=[
            pl.BlockSpec((block, rows, width), lambda i: (i, 0, 0)),
            pl.BlockSpec(courant.shape, lambda i: (0, 0, 0)),
        ],
        out_specs=[spec, spec],
        out_shape=[shape, shape],
        cost_estimate=cost(1000, 6 << 20),
        compiler_params=params(),
    )(field, courant)


def edge_weights(halo, groups):
    return jnp.sum(halo[0, groups:groups + 12].astype(jnp.float32).reshape(3, 4, 1, -1), axis=0)


def stepper(coef_ref, offset, delta, width):
    def step(r, south, center, north):
        east = pltpu.roll(center, width - 1, 1)
        west = pltpu.roll(center, 1, 1)
        at = r + offset
        c = [coef_ref[k, at:at + 1, :] for k in range(5)]
        pulse = jnp.where(delta == r * width, 1.0, 0.0)
        return c[4] * center + c[0] * north + c[1] * south + c[2] * east + c[3] * west + pulse

    return step


def offsets(det_ref, at, first_cell, width):
    return det_ref[at, :] - first_cell - lax.broadcasted_iota(jnp.int32, (16, width), 1)


def put(keep_ref, send_ref, at, p, own_first, low, high):
    width = low.shape[1]
    cols = pl.ds(p * width, width)
    keep_ref[at, cols] = jnp.where(own_first, low, high).astype(BF)
    send_ref[at, cols] = jnp.where(own_first, high, low).astype(BF)


def inner_kernel(info, x_ref, coef_ref, emis_ref, det_ref, adv_ref, keep_ref, send_ref):
    block, rows, width = x_ref.shape
    own_first = info[1] == 0

    def group(g, carry):
        at = pl.ds(pl.multiple_of(g * 16, 16), 16)
        step = stepper(coef_ref, 0, offsets(det_ref, at, info[2], width), width)
        v = jnp.swapaxes(x_ref[at], 0, 1)
        first = {r: step(r, v[r - 1], v[r], v[r + 1]) for r in range(1, rows - 1)}
        out = {r: step(r, first[r - 1], first[r], first[r + 1]) for r in range(2, rows - 2)}
        tile = jnp.stack([out[min(max(r, 2), rows - 3)] for r in range(rows)])
        adv_ref[at] = jnp.swapaxes(tile, 0, 1)
        prints = {r: out[r] * emis_ref[r:r + 1, :] for r in out}
        for p in range(2):
            put(keep_ref, send_ref, at, p, own_first, prints[p + 2], prints[p + 4])
        return carry

    lax.fori_loop(0, block // 16, group, 0, unroll=2)


def outer_kernel(info, x_ref, up_ref, down_ref, coef_ref, emis_ref, det_ref, mid_ref, adv_ref, keep_ref, send_ref):
    block, rows, width = x_ref.shape
    own_first = info[1] == 0

    def group(g, carry):
        at = pl.ds(pl.multiple_of(g * 16, 16), 16)
        step = stepper(coef_ref, 1, offsets(det_ref, at, info[2], width), width)
        tile = jnp.swapaxes(x_ref[at], 0, 1)
        v = {r: tile[r] for r in range(rows)}
        for r in range(2):
            v[r - 2] = up_ref[r, at, :].astype(jnp.float32)
            v[r + rows] = down_ref[r, at, :].astype(jnp.float32)
        first = {r: step(r, v[r - 1], v[r], v[r + 1]) for r in (-1, 0, 1, 2, 5, 6, 7, 8)}
        out = {r: step(r, first[r - 1], first[r], first[r + 1]) for r in (0, 1, 6, 7)}
        tile = jnp.stack([out[r if r in out else (1 if r < 4 else 6)] for r in range(rows)])
        tile = jnp.swapaxes(tile, 0, 1)
        row = lax.broadcasted_iota(jnp.int32, tile.shape, 1)
        adv_ref[at] = jnp.where((row >= 2) & (row < 6), mid_ref[at], tile)
        prints = {r: out[r] * emis_ref[r:r + 1, :] for r in out}
        for p in range(2):
            put(keep_ref, send_ref, at, p, own_first, prints[p], prints[p + 6])
        return carry

    lax.fori_loop(0, block // 16, group, 0, unroll=2)


def stencil(kernel, info, field, halos, coef, emis, det, mid, work):
    groups, rows, width = field.shape
    block = 64
    count = groups // block
    half = count // 2
    cells = 2 * width

    def turned(i, info):
        return lax.rem(i + info[0] * half, count)

    fields = pl.BlockSpec((block, rows, width), lambda i, info: (turned(i, info), 0, 0))
    halo = pl.BlockSpec((2, block, width), lambda i, info: (0, turned(i, info), 0))
    prints = pl.BlockSpec((block, cells), lambda i, info: (i, 0))
    print_shape = jax.ShapeDtypeStruct((groups, cells), BF)
    operands = [field, *halos, coef, emis, det, *mid]
    return pl.pallas_call(
        kernel,
        grid_spec=pltpu.PrefetchScalarGridSpec(
            num_scalar_prefetch=1,
            grid=(count,),
            in_specs=[
                fields,
                *([halo] * len(halos)),
                pl.BlockSpec(coef.shape, lambda i, info: (0, 0, 0)),
                pl.BlockSpec((rows, width), lambda i, info: (0, 0)),
                pl.BlockSpec((block, 1), lambda i, info: (turned(i, info), 0)),
                *([fields] * len(mid)),
            ],
            out_specs=[fields, prints, prints],
        ),
        out_shape=[jax.ShapeDtypeStruct(field.shape, jnp.float32), print_shape, print_shape],
        input_output_aliases={len(operands): 0} if mid else {},
        cost_estimate=cost(1000, work),
        compiler_params=params(),
    )(info, *operands)


NT = (((1,), (1,)), ((), ()))


def dot(left, right):
    return lax.dot_general(left, right, NT, preferred_element_type=jnp.float32)


def gram_kernel(grows, info, *refs):
    stack, outs = refs[-1], refs[-3:-1]
    accs = refs[12:14] if grows else None
    own, own_s, nxt, nxt_s, last, last_s = (refs[2 * k:2 * k + 2] for k in range(6))
    core, xl, y, xpos, z = info[0], info[1], info[3], info[4], info[5]
    rows = nxt_s[0].shape[0]
    half = own[0].shape[1]
    part = rows // 2
    lefts = []
    for e, tile, sibling, first in ((1, nxt, nxt_s, 0), (0, own, own_s, rows), (3, last, last_s, rows)):
        for i in range(2):
            at = pl.ds(len(lefts) * rows, rows)
            stack[at, :half] = tile[i][:rows, :]
            stack[at, half:] = sibling[i][first:first + rows, :]
            lefts.append((e, i))

    for j in range(2):
        for m in range(2):
            mine = slice(m * rows, (m + 1) * rows)
            theirs = slice((1 - m) * rows, (2 - m) * rows)
            here = dot(stack[:, :half], own[j][mine, :]) + dot(stack[:, half:], own_s[j][theirs, :])
            far = dot(stack[:2 * rows, :half], last[j][mine, :]) + dot(
                stack[:2 * rows, half:], last_s[j][theirs, :]
            )
            cols = pl.ds(pl.multiple_of(lax.rem(core + m, 2) * rows, rows), rows)
            values = [(e, i, here[k * rows:(k + 1) * rows]) for k, (e, i) in enumerate(lefts)]
            values += [(2, i, far[i * rows:(i + 1) * rows]) for i in range(2)]
            for e, i, value in values:
                at_z = lax.rem(y + e, 4)
                at_x = lax.rem(lax.rem(i + xl, 2) * 2 + lax.rem(j + xl, 2) + 4 - xpos, 4)
                from_z = lax.rem(at_z + 4 - z, 4)
                for upper, slot in enumerate((from_z * 4 + at_x, at_x * 4 + at_z)):
                    piece = value[upper * part:(upper + 1) * part]
                    if accs is not None:
                        piece = piece + accs[upper][slot, :, cols]
                    outs[upper][slot, :, cols] = piece


def partial_gram(info, operands, acc):
    rows, half = operands[0].shape
    rows = rows // 2
    whole = pl.BlockSpec(memory_space=pltpu.VMEM)
    shape = jax.ShapeDtypeStruct((16, rows // 2, 2 * rows), jnp.float32)
    return pl.pallas_call(
        lambda *refs: gram_kernel(bool(acc), *refs),
        in_specs=[pl.BlockSpec(memory_space=pltpu.SMEM)] + [whole] * (len(operands) + len(acc)),
        out_specs=[whole, whole],
        out_shape=[shape, shape],
        scratch_shapes=[pltpu.VMEM((6 * rows, 2 * half), BF)],
        cost_estimate=cost(1000, 8 << 20),
        compiler_params=params(),
    )(info, *operands, *acc)


def to_four(pieces, axis):
    total = pieces[0].astype(jnp.float32)
    for d in (1, 2, 3):
        came = lax.ppermute(pieces[d], axis, [(i, (i + d) % 4) for i in range(4)])
        total = total + came.astype(jnp.float32)
    return total * 0.25


def after(value, *others):
    return lax.optimization_barrier((value, others))[0]


def along_y(own):
    nxt = lax.ppermute(own, "y", [((i + 1) % 4, i) for i in range(4)])
    last = lax.ppermute(own, "y", [(i, (i + 1) % 4) for i in range(4)])
    return nxt, last


def siblings(own, nxt, last):
    part = own.shape[0] // 2
    own_s = lax.ppermute(own, "core", SWAP)
    nxt_s = lax.ppermute(nxt[part:], "core", SWAP)
    last_s = lax.ppermute(last, "core", SWAP)
    return own, own_s, nxt, nxt_s, last, last_s


def gram_operands(keep, keep_y, other, other_y):
    return [
        array for pair in zip(siblings(keep, *keep_y), siblings(other, *other_y)) for array in pair
    ]


def mean_of_four(pieces):
    return jnp.sum(pieces.astype(jnp.float32), axis=0) * 0.25


def body(adjoint, courant, detector, sources, emission):
    groups, rows, width = adjoint.shape
    core = lax.axis_index("core")
    xl = lax.axis_index("xl")
    y = lax.axis_index("y")
    z = lax.axis_index("z")
    tile = lax.axis_index(GRID)
    first_cell = tile * rows * width
    xpos = lax.axis_index(XS)
    info = jnp.stack([core, xl, first_cell, y, xpos, z]).astype(jnp.int32)
    count = lax.axis_size(GRID)
    forward = [(i, i + 1) for i in range(count - 1)]
    backward = [(i + 1, i) for i in range(count - 1)]

    top, bottom = edges(adjoint, courant)
    up = lax.ppermute(bottom, GRID, forward)
    down = lax.ppermute(top, GRID, backward)
    columns = jnp.arange(width)

    def weights(c):
        return jnp.stack([
            c[0],
            c[1],
            jnp.where(columns == width - 1, 0.0, c[2]),
            jnp.where(columns == 0, 0.0, c[3]),
            1.0 - (c[0] + c[1] + c[2] + c[3]),
        ])

    local = sources - first_cell
    by_row = jnp.where(
        (local // width)[None, :] == jnp.arange(rows)[:, None], emission[None, :], 0.0
    )
    by_col = ((local % width)[:, None] == columns[None, :]).astype(jnp.float32)
    emis = jnp.dot(by_row, by_col, precision=lax.Precision.HIGHEST)
    det = detector[:, None]

    weights_in = weights(courant)
    mid, keep, send = stencil(
        inner_kernel, after(info, top, bottom), adjoint, [], weights_in, emis, det, [], INNER
    )
    other = lax.ppermute(send, "xl", SWAP)
    keep_y = along_y(after(keep, up, down))
    other_y = along_y(after(other, keep_y))
    totals = partial_gram(info, gram_operands(keep, keep_y, other, other_y), [])

    extended = jnp.concatenate(
        [edge_weights(up, groups), courant, edge_weights(down, groups)], axis=1
    )
    field, keep, send = stencil(
        outer_kernel, after(info, keep_y), adjoint, [up, down], weights(extended), emis, det,
        [mid], OUTER
    )
    other = lax.ppermute(send, "xl", SWAP)
    keep_y = along_y(keep)
    other_y = along_y(after(other, keep_y, totals))
    totals = partial_gram(info, gram_operands(keep, keep_y, other, other_y), totals)

    along_z, along_x = [
        (total * LIFT).astype(HALF).reshape(4, 4, groups // 4, groups) for total in totals
    ]
    along_x = to_four(along_x, XS).astype(HALF)
    along_z = to_four(along_z, "z").astype(HALF)
    along_x = mean_of_four(lax.all_to_all(along_x, "z", 0, 0, tiled=True))
    along_z = to_four(along_z, XS)
    summed = jnp.concatenate([along_z, along_x], axis=0)
    moves = [((i + 2) % 4 * 4 + i, (i + 1) % 4 * 4 + (i + 3) % 4) for i in range(4)]
    moved = lax.ppermute(summed.astype(HALF), ("z", "y"), moves).astype(jnp.float32)
    summed = jnp.where(lax.rem(y + 2, 4) == z, moved, summed)
    total_sources = sources.shape[0] * count
    return field, summed * jnp.float32(16.0 / (LIFT * total_sources))


def solution(mesh):
    fine = Mesh(mesh.devices.reshape(4, 2, 2, 4, 2), ("z", "xh", "core", "y", "xl"))
    rec = ("y", "xl")
    in_specs = (P(rec, GRID, None), P(None, GRID, None), P(rec), P(GRID), P(GRID))
    out_specs = (P(rec, GRID, None), P(GRID, rec))
    return jax.shard_map(body, mesh=fine, in_specs=in_specs, out_specs=out_specs, check_vma=False)
```

```python
import jax
import jax.numpy as jnp
from jax import lax
from jax.experimental import pallas as pl
from jax.experimental.pallas import tpu as pltpu
from jax.sharding import Mesh, PartitionSpec as P

GRID = ("z", "xh", "core")
XS = ("xh", "xl")
HALF = jnp.float16
BF = jnp.bfloat16
VMEM_LIMIT = 16 * 1024 * 1024
LIFT = 1.0 / 256
SWAP = [(0, 1), (1, 0)]
INNER = 100 << 20
OUTER = 20 << 20


def params():
    return pltpu.CompilerParams(vmem_limit_bytes=VMEM_LIMIT)


def cost(flops, moved):
    return pl.CostEstimate(flops=flops, bytes_accessed=moved, transcendentals=0)


def edge_kernel(x_ref, c_ref, top_ref, bot_ref):
    i = pl.program_id(0)
    block, rows, _ = x_ref.shape
    at = pl.ds(pl.multiple_of(i * block, block), block)
    for out_ref, first, edge in ((top_ref, 0, 0), (bot_ref, rows - 2, rows - 1)):
        out_ref[0, at, :] = x_ref[:, first, :].astype(BF)
        out_ref[1, at, :] = x_ref[:, first + 1, :].astype(BF)

        @pl.when(i == 0)
        def _():
            rest = c_ref[:, edge, :]
            terms = []
            for _ in range(3):
                terms.append(rest.astype(BF).astype(jnp.float32))
                rest = rest - terms[-1]
            packed = jnp.concatenate(terms + [jnp.zeros_like(rest)], axis=0).astype(BF)
            last = out_ref.shape[1] - packed.shape[0]
            for k in range(2):
                out_ref[k, last:, :] = packed


def edges(field, courant):
    groups, rows, width = field.shape
    block = 64
    shape = jax.ShapeDtypeStruct((2, groups + 16, width), BF)
    spec = pl.BlockSpec(shape.shape, lambda i: (0, 0, 0))
    return pl.pallas_call(
        edge_kernel,
        grid=(groups // block,),
        in_specs=[
            pl.BlockSpec((block, rows, width), lambda i: (i, 0, 0)),
            pl.BlockSpec(courant.shape, lambda i: (0, 0, 0)),
        ],
        out_specs=[spec, spec],
        out_shape=[shape, shape],
        cost_estimate=cost(1000, 6 << 20),
        compiler_params=params(),
    )(field, courant)


def edge_weights(halo, groups):
    return jnp.sum(halo[0, groups:groups + 12].astype(jnp.float32).reshape(3, 4, 1, -1), axis=0)


def stepper(coef_ref, offset, delta, width):
    def step(r, south, center, north):
        east = pltpu.roll(center, width - 1, 1)
        west = pltpu.roll(center, 1, 1)
        at = r + offset
        c = [coef_ref[k, at:at + 1, :] for k in range(5)]
        pulse = jnp.where(delta == r * width, 1.0, 0.0)
        return c[4] * center + c[0] * north + c[1] * south + c[2] * east + c[3] * west + pulse

    return step


def offsets(det_ref, at, first_cell, width):
    return det_ref[at, :] - first_cell - lax.broadcasted_iota(jnp.int32, (16, width), 1)


def put(keep_ref, send_ref, at, p, own_first, low, high):
    width = low.shape[1]
    cols = pl.ds(p * width, width)
    keep_ref[at, cols] = jnp.where(own_first, low, high).astype(BF)
    send_ref[at, cols] = jnp.where(own_first, high, low).astype(BF)


def inner_kernel(info, x_ref, coef_ref, emis_ref, det_ref, adv_ref, keep_ref, send_ref):
    block, rows, width = x_ref.shape
    own_first = info[1] == 0

    def group(g, carry):
        at = pl.ds(pl.multiple_of(g * 16, 16), 16)
        step = stepper(coef_ref, 0, offsets(det_ref, at, info[2], width), width)
        v = jnp.swapaxes(x_ref[at], 0, 1)
        first = {r: step(r, v[r - 1], v[r], v[r + 1]) for r in range(1, rows - 1)}
        out = {r: step(r, first[r - 1], first[r], first[r + 1]) for r in range(2, rows - 2)}
        tile = jnp.stack([out[min(max(r, 2), rows - 3)] for r in range(rows)])
        adv_ref[at] = jnp.swapaxes(tile, 0, 1)
        prints = {r: out[r] * emis_ref[r:r + 1, :] for r in out}
        for p in range(2):
            put(keep_ref, send_ref, at, p, own_first, prints[p + 2], prints[p + 4])
        return carry

    lax.fori_loop(0, block // 16, group, 0, unroll=2)


def outer_kernel(info, x_ref, up_ref, down_ref, coef_ref, emis_ref, det_ref, mid_ref, adv_ref, keep_ref, send_ref):
    block, rows, width = x_ref.shape
    own_first = info[1] == 0

    def group(g, carry):
        at = pl.ds(pl.multiple_of(g * 16, 16), 16)
        step = stepper(coef_ref, 1, offsets(det_ref, at, info[2], width), width)
        tile = jnp.swapaxes(x_ref[at], 0, 1)
        v = {r: tile[r] for r in range(rows)}
        for r in range(2):
            v[r - 2] = up_ref[r, at, :].astype(jnp.float32)
            v[r + rows] = down_ref[r, at, :].astype(jnp.float32)
        first = {r: step(r, v[r - 1], v[r], v[r + 1]) for r in (-1, 0, 1, 2, 5, 6, 7, 8)}
        out = {r: step(r, first[r - 1], first[r], first[r + 1]) for r in (0, 1, 6, 7)}
        tile = jnp.stack([out[r if r in out else (1 if r < 4 else 6)] for r in range(rows)])
        tile = jnp.swapaxes(tile, 0, 1)
        row = lax.broadcasted_iota(jnp.int32, tile.shape, 1)
        adv_ref[at] = jnp.where((row >= 2) & (row < 6), mid_ref[at], tile)
        prints = {r: out[r] * emis_ref[r:r + 1, :] for r in out}
        for p in range(2):
            put(keep_ref, send_ref, at, p, own_first, prints[p], prints[p + 6])
        return carry

    lax.fori_loop(0, block // 16, group, 0, unroll=2)


def stencil(kernel, info, field, halos, coef, emis, det, mid, work):
    groups, rows, width = field.shape
    block = 64
    count = groups // block
    half = count // 2
    cells = 2 * width

    def turned(i, info):
        return lax.rem(i + info[0] * half, count)

    fields = pl.BlockSpec((block, rows, width), lambda i, info: (turned(i, info), 0, 0))
    halo = pl.BlockSpec((2, block, width), lambda i, info: (0, turned(i, info), 0))
    prints = pl.BlockSpec((block, cells), lambda i, info: (i, 0))
    print_shape = jax.ShapeDtypeStruct((groups, cells), BF)
    operands = [field, *halos, coef, emis, det, *mid]
    return pl.pallas_call(
        kernel,
        grid_spec=pltpu.PrefetchScalarGridSpec(
            num_scalar_prefetch=1,
            grid=(count,),
            in_specs=[
                fields,
                *([halo] * len(halos)),
                pl.BlockSpec(coef.shape, lambda i, info: (0, 0, 0)),
                pl.BlockSpec((rows, width), lambda i, info: (0, 0)),
                pl.BlockSpec((block, 1), lambda i, info: (turned(i, info), 0)),
                *([fields] * len(mid)),
            ],
            out_specs=[fields, prints, prints],
        ),
        out_shape=[jax.ShapeDtypeStruct(field.shape, jnp.float32), print_shape, print_shape],
        input_output_aliases={len(operands): 0} if mid else {},
        cost_estimate=cost(1000, work),
        compiler_params=params(),
    )(info, *operands)


NT = (((1,), (1,)), ((), ()))


def dot(left, right):
    return lax.dot_general(left, right, NT, preferred_element_type=jnp.float32)


def gram_kernel(grows, info, *refs):
    stack, outs = refs[-1], refs[-3:-1]
    accs = refs[12:14] if grows else None
    own, own_s, nxt, nxt_s, last, last_s = (refs[2 * k:2 * k + 2] for k in range(6))
    core, xl, y, xpos, z = info[0], info[1], info[3], info[4], info[5]
    rows = nxt_s[0].shape[0]
    half = own[0].shape[1]
    part = rows // 2
    lefts = []
    for e, tile, sibling, first in ((1, nxt, nxt_s, 0), (0, own, own_s, rows), (3, last, last_s, rows)):
        for i in range(2):
            at = pl.ds(len(lefts) * rows, rows)
            stack[at, :half] = tile[i][:rows, :]
            stack[at, half:] = sibling[i][first:first + rows, :]
            lefts.append((e, i))

    for j in range(2):
        for m in range(2):
            mine = slice(m * rows, (m + 1) * rows)
            theirs = slice((1 - m) * rows, (2 - m) * rows)
            here = dot(stack[:, :half], own[j][mine, :]) + dot(stack[:, half:], own_s[j][theirs, :])
            far = dot(stack[:2 * rows, :half], last[j][mine, :]) + dot(
                stack[:2 * rows, half:], last_s[j][theirs, :]
            )
            cols = pl.ds(pl.multiple_of(lax.rem(core + m, 2) * rows, rows), rows)
            values = [(e, i, here[k * rows:(k + 1) * rows]) for k, (e, i) in enumerate(lefts)]
            values += [(2, i, far[i * rows:(i + 1) * rows]) for i in range(2)]
            for e, i, value in values:
                at_z = lax.rem(y + e, 4)
                at_x = lax.rem(lax.rem(i + xl, 2) * 2 + lax.rem(j + xl, 2) + 4 - xpos, 4)
                from_z = lax.rem(at_z + 4 - z, 4)
                for upper, slot in enumerate((from_z * 4 + at_x, at_x * 4 + at_z)):
                    piece = value[upper * part:(upper + 1) * part]
                    if accs is not None:
                        piece = piece + accs[upper][slot, :, cols]
                    outs[upper][slot, :, cols] = piece


def partial_gram(info, operands, acc):
    rows, half = operands[0].shape
    rows = rows // 2
    whole = pl.BlockSpec(memory_space=pltpu.VMEM)
    shape = jax.ShapeDtypeStruct((16, rows // 2, 2 * rows), jnp.float32)
    return pl.pallas_call(
        lambda *refs: gram_kernel(bool(acc), *refs),
        in_specs=[pl.BlockSpec(memory_space=pltpu.SMEM)] + [whole] * (len(operands) + len(acc)),
        out_specs=[whole, whole],
        out_shape=[shape, shape],
        scratch_shapes=[pltpu.VMEM((6 * rows, 2 * half), BF)],
        cost_estimate=cost(1000, 8 << 20),
        compiler_params=params(),
    )(info, *operands, *acc)


def place(z, y, x):
    return ((z % 4 * 2 + x % 4 // 2) * 4 + y % 4) * 2 + x % 2


def to_places(pieces):
    z, y = lax.axis_index("z"), lax.axis_index("y")
    total = 0.0
    for d in range(4):
        pairs = []
        for zi in range(4):
            for yi in range(4):
                moves = (zi - yi) % 4 == 2
                if moves or d:
                    pairs += [
                        (place(zi, yi, xi), place(zi - moves, yi - moves, xi + d)) for xi in range(4)
                    ]
        came = lax.ppermute(pieces[d], ("z", "xh", "y", "xl"), pairs)
        if d == 0:
            came = jnp.where(lax.rem(y + 2, 4) == z, came, pieces[0])
        total = total + came.astype(jnp.float32)
    return total * 0.25


def to_four(pieces, axis):
    total = pieces[0].astype(jnp.float32)
    for d in (1, 2, 3):
        came = lax.ppermute(pieces[d], axis, [(i, (i + d) % 4) for i in range(4)])
        total = total + came.astype(jnp.float32)
    return total * 0.25


def after(value, *others):
    return lax.optimization_barrier((value, others))[0]


def along_y(own):
    nxt = lax.ppermute(own, "y", [((i + 1) % 4, i) for i in range(4)])
    last = lax.ppermute(own, "y", [(i, (i + 1) % 4) for i in range(4)])
    return nxt, last


def siblings(own, nxt, last):
    part = own.shape[0] // 2
    own_s = lax.ppermute(own, "core", SWAP)
    nxt_s = lax.ppermute(nxt[part:], "core", SWAP)
    last_s = lax.ppermute(last, "core", SWAP)
    return own, own_s, nxt, nxt_s, last, last_s


def gram_operands(keep, keep_y, other, other_y):
    return [
        array for pair in zip(siblings(keep, *keep_y), siblings(other, *other_y)) for array in pair
    ]


def mean_of_four(pieces):
    return jnp.sum(pieces.astype(jnp.float32), axis=0) * 0.25


def body(adjoint, courant, detector, sources, emission):
    groups, rows, width = adjoint.shape
    core = lax.axis_index("core")
    xl = lax.axis_index("xl")
    y = lax.axis_index("y")
    z = lax.axis_index("z")
    tile = lax.axis_index(GRID)
    first_cell = tile * rows * width
    xpos = lax.axis_index(XS)
    info = jnp.stack([core, xl, first_cell, y, xpos, z]).astype(jnp.int32)
    count = lax.axis_size(GRID)
    forward = [(i, i + 1) for i in range(count - 1)]
    backward = [(i + 1, i) for i in range(count - 1)]

    top, bottom = edges(adjoint, courant)
    up = lax.ppermute(bottom, GRID, forward)
    down = lax.ppermute(top, GRID, backward)
    columns = jnp.arange(width)

    def weights(c):
        return jnp.stack([
            c[0],
            c[1],
            jnp.where(columns == width - 1, 0.0, c[2]),
            jnp.where(columns == 0, 0.0, c[3]),
            1.0 - (c[0] + c[1] + c[2] + c[3]),
        ])

    local = sources - first_cell
    by_row = jnp.where(
        (local // width)[None, :] == jnp.arange(rows)[:, None], emission[None, :], 0.0
    )
    by_col = ((local % width)[:, None] == columns[None, :]).astype(jnp.float32)
    emis = jnp.dot(by_row, by_col, precision=lax.Precision.HIGHEST)
    det = detector[:, None]

    weights_in = weights(courant)
    mid, keep, send = stencil(
        inner_kernel, after(info, top, bottom), adjoint, [], weights_in, emis, det, [], INNER
    )
    other = lax.ppermute(send, "xl", SWAP)
    keep_y = along_y(after(keep, up, down))
    other_y = along_y(after(other, keep_y))
    totals = partial_gram(info, gram_operands(keep, keep_y, other, other_y), [])

    extended = jnp.concatenate(
        [edge_weights(up, groups), courant, edge_weights(down, groups)], axis=1
    )
    field, keep, send = stencil(
        outer_kernel, after(info, keep_y), adjoint, [up, down], weights(extended), emis, det,
        [mid], OUTER
    )
    other = lax.ppermute(send, "xl", SWAP)
    keep_y = along_y(keep)
    other_y = along_y(after(other, keep_y, totals))
    totals = partial_gram(info, gram_operands(keep, keep_y, other, other_y), totals)

    along_z, along_x = [
        (total * LIFT).astype(HALF).reshape(4, 4, groups // 4, groups) for total in totals
    ]
    along_x = to_four(along_x, XS).astype(HALF)
    along_z = to_four(along_z, "z").astype(HALF)
    along_x = mean_of_four(lax.all_to_all(along_x, "z", 0, 0, tiled=True))
    moves = [((i + 2) % 4 * 4 + i, (i + 1) % 4 * 4 + (i + 3) % 4) for i in range(4)]
    moved = lax.ppermute(along_x.astype(HALF), ("z", "y"), moves).astype(jnp.float32)
    along_x = jnp.where(lax.rem(y + 2, 4) == z, moved, along_x)
    summed = jnp.concatenate([to_places(along_z), along_x], axis=0)
    total_sources = sources.shape[0] * count
    return field, summed * jnp.float32(16.0 / (LIFT * total_sources))


def solution(mesh):
    fine = Mesh(mesh.devices.reshape(4, 2, 2, 4, 2), ("z", "xh", "core", "y", "xl"))
    rec = ("y", "xl")
    in_specs = (P(rec, GRID, None), P(None, GRID, None), P(rec), P(GRID), P(GRID))
    out_specs = (P(rec, GRID, None), P(GRID, rec))
    return jax.shard_map(body, mesh=fine, in_specs=in_specs, out_specs=out_specs, check_vma=False)
```

```python
import jax
import jax.numpy as jnp
from jax import lax
from jax.experimental import pallas as pl
from jax.experimental.pallas import tpu as pltpu
from jax.sharding import Mesh, PartitionSpec as P

GRID = ("z", "xh", "core")
XS = ("xh", "xl")
HALF = jnp.float16
BF = jnp.bfloat16
VMEM_LIMIT = 16 * 1024 * 1024
LIFT = 1.0 / 256
SWAP = [(0, 1), (1, 0)]
INNER = 100 << 20
OUTER = 20 << 20


def params():
    return pltpu.CompilerParams(vmem_limit_bytes=VMEM_LIMIT)


def cost(flops, moved):
    return pl.CostEstimate(flops=flops, bytes_accessed=moved, transcendentals=0)


def edge_kernel(x_ref, c_ref, top_ref, bot_ref):
    i = pl.program_id(0)
    block, rows, _ = x_ref.shape
    at = pl.ds(pl.multiple_of(i * block, block), block)
    for out_ref, first, edge in ((top_ref, 0, 0), (bot_ref, rows - 2, rows - 1)):
        out_ref[0, at, :] = x_ref[:, first, :].astype(BF)
        out_ref[1, at, :] = x_ref[:, first + 1, :].astype(BF)

        @pl.when(i == 0)
        def _():
            rest = c_ref[:, edge, :]
            terms = []
            for _ in range(3):
                terms.append(rest.astype(BF).astype(jnp.float32))
                rest = rest - terms[-1]
            packed = jnp.concatenate(terms + [jnp.zeros_like(rest)], axis=0).astype(BF)
            last = out_ref.shape[1] - packed.shape[0]
            for k in range(2):
                out_ref[k, last:, :] = packed


def edges(field, courant):
    groups, rows, width = field.shape
    block = 64
    shape = jax.ShapeDtypeStruct((2, groups + 16, width), BF)
    spec = pl.BlockSpec(shape.shape, lambda i: (0, 0, 0))
    return pl.pallas_call(
        edge_kernel,
        grid=(groups // block,),
        in_specs=[
            pl.BlockSpec((block, rows, width), lambda i: (i, 0, 0)),
            pl.BlockSpec(courant.shape, lambda i: (0, 0, 0)),
        ],
        out_specs=[spec, spec],
        out_shape=[shape, shape],
        cost_estimate=cost(1000, 6 << 20),
        compiler_params=params(),
    )(field, courant)


def edge_weights(halo, groups):
    return jnp.sum(halo[0, groups:groups + 12].astype(jnp.float32).reshape(3, 4, 1, -1), axis=0)


def stepper(coef_ref, offset, delta, width):
    def step(r, south, center, north):
        east = pltpu.roll(center, width - 1, 1)
        west = pltpu.roll(center, 1, 1)
        at = r + offset
        c = [coef_ref[k, at:at + 1, :] for k in range(5)]
        pulse = jnp.where(delta == r * width, 1.0, 0.0)
        return c[4] * center + c[0] * north + c[1] * south + c[2] * east + c[3] * west + pulse

    return step


def offsets(det_ref, at, first_cell, width):
    return det_ref[at, :] - first_cell - lax.broadcasted_iota(jnp.int32, (16, width), 1)


def put(keep_ref, send_ref, at, p, own_first, low, high):
    width = low.shape[1]
    cols = pl.ds(p * width, width)
    keep_ref[at, cols] = jnp.where(own_first, low, high).astype(BF)
    send_ref[at, cols] = jnp.where(own_first, high, low).astype(BF)


def inner_kernel(info, x_ref, coef_ref, emis_ref, det_ref, adv_ref, keep_ref, send_ref):
    block, rows, width = x_ref.shape
    own_first = info[1] == 0

    def group(g, carry):
        at = pl.ds(pl.multiple_of(g * 16, 16), 16)
        step = stepper(coef_ref, 0, offsets(det_ref, at, info[2], width), width)
        v = jnp.swapaxes(x_ref[at], 0, 1)
        first = {r: step(r, v[r - 1], v[r], v[r + 1]) for r in range(1, rows - 1)}
        out = {r: step(r, first[r - 1], first[r], first[r + 1]) for r in range(2, rows - 2)}
        tile = jnp.stack([out[min(max(r, 2), rows - 3)] for r in range(rows)])
        adv_ref[at] = jnp.swapaxes(tile, 0, 1)
        prints = {r: out[r] * emis_ref[r:r + 1, :] for r in out}
        for p in range(2):
            put(keep_ref, send_ref, at, p, own_first, prints[p + 2], prints[p + 4])
        return carry

    lax.fori_loop(0, block // 16, group, 0, unroll=2)


def outer_kernel(info, x_ref, up_ref, down_ref, coef_ref, emis_ref, det_ref, mid_ref, adv_ref, keep_ref, send_ref):
    block, rows, width = x_ref.shape
    own_first = info[1] == 0

    def group(g, carry):
        at = pl.ds(pl.multiple_of(g * 16, 16), 16)
        step = stepper(coef_ref, 1, offsets(det_ref, at, info[2], width), width)
        tile = jnp.swapaxes(x_ref[at], 0, 1)
        v = {r: tile[r] for r in range(rows)}
        for r in range(2):
            v[r - 2] = up_ref[r, at, :].astype(jnp.float32)
            v[r + rows] = down_ref[r, at, :].astype(jnp.float32)
        first = {r: step(r, v[r - 1], v[r], v[r + 1]) for r in (-1, 0, 1, 2, 5, 6, 7, 8)}
        out = {r: step(r, first[r - 1], first[r], first[r + 1]) for r in (0, 1, 6, 7)}
        tile = jnp.stack([out[r if r in out else (1 if r < 4 else 6)] for r in range(rows)])
        tile = jnp.swapaxes(tile, 0, 1)
        row = lax.broadcasted_iota(jnp.int32, tile.shape, 1)
        adv_ref[at] = jnp.where((row >= 2) & (row < 6), mid_ref[at], tile)
        prints = {r: out[r] * emis_ref[r:r + 1, :] for r in out}
        for p in range(2):
            put(keep_ref, send_ref, at, p, own_first, prints[p], prints[p + 6])
        return carry

    lax.fori_loop(0, block // 16, group, 0, unroll=2)


def stencil(kernel, info, field, halos, coef, emis, det, mid, work):
    groups, rows, width = field.shape
    block = 64
    count = groups // block
    half = count // 2
    cells = 2 * width

    def turned(i, info):
        return lax.rem(i + info[0] * half, count)

    fields = pl.BlockSpec((block, rows, width), lambda i, info: (turned(i, info), 0, 0))
    halo = pl.BlockSpec((2, block, width), lambda i, info: (0, turned(i, info), 0))
    prints = pl.BlockSpec((block, cells), lambda i, info: (i, 0))
    print_shape = jax.ShapeDtypeStruct((groups, cells), BF)
    operands = [field, *halos, coef, emis, det, *mid]
    return pl.pallas_call(
        kernel,
        grid_spec=pltpu.PrefetchScalarGridSpec(
            num_scalar_prefetch=1,
            grid=(count,),
            in_specs=[
                fields,
                *([halo] * len(halos)),
                pl.BlockSpec(coef.shape, lambda i, info: (0, 0, 0)),
                pl.BlockSpec((rows, width), lambda i, info: (0, 0)),
                pl.BlockSpec((block, 1), lambda i, info: (turned(i, info), 0)),
                *([fields] * len(mid)),
            ],
            out_specs=[fields, prints, prints],
        ),
        out_shape=[jax.ShapeDtypeStruct(field.shape, jnp.float32), print_shape, print_shape],
        input_output_aliases={len(operands): 0} if mid else {},
        cost_estimate=cost(1000, work),
        compiler_params=params(),
    )(info, *operands)


NT = (((1,), (1,)), ((), ()))


def dot(left, right):
    return lax.dot_general(left, right, NT, preferred_element_type=jnp.float32)


def gram_kernel(grows, info, *refs):
    stack, outs = refs[-1], refs[-3:-1]
    accs = refs[12:14] if grows else None
    own, own_s, nxt, nxt_s, last, last_s = (refs[2 * k:2 * k + 2] for k in range(6))
    core, xl, y, xpos, z = info[0], info[1], info[3], info[4], info[5]
    rows = nxt_s[0].shape[0]
    half = own[0].shape[1]
    part = rows // 2
    lefts = []
    for e, tile, sibling, first in ((1, nxt, nxt_s, 0), (0, own, own_s, rows), (3, last, last_s, rows)):
        for i in range(2):
            at = pl.ds(len(lefts) * rows, rows)
            stack[at, :half] = tile[i][:rows, :]
            stack[at, half:] = sibling[i][first:first + rows, :]
            lefts.append((e, i))

    for j in range(2):
        for m in range(2):
            mine = slice(m * rows, (m + 1) * rows)
            theirs = slice((1 - m) * rows, (2 - m) * rows)
            here = dot(stack[:, :half], own[j][mine, :]) + dot(stack[:, half:], own_s[j][theirs, :])
            far = dot(stack[:2 * rows, :half], last[j][mine, :]) + dot(
                stack[:2 * rows, half:], last_s[j][theirs, :]
            )
            cols = pl.ds(pl.multiple_of(lax.rem(core + m, 2) * rows, rows), rows)
            values = [(e, i, here[k * rows:(k + 1) * rows]) for k, (e, i) in enumerate(lefts)]
            values += [(2, i, far[i * rows:(i + 1) * rows]) for i in range(2)]
            for e, i, value in values:
                at_z = lax.rem(y + e, 4)
                at_x = lax.rem(lax.rem(i + xl, 2) * 2 + lax.rem(j + xl, 2) + 4 - xpos, 4)
                from_z = lax.rem(at_z + 4 - z, 4)
                for upper, slot in enumerate((from_z * 4 + at_x, at_x * 4 + at_z)):
                    piece = value[upper * part:(upper + 1) * part]
                    if accs is not None:
                        piece = piece + accs[upper][slot, :, cols]
                    outs[upper][slot, :, cols] = piece


def partial_gram(info, operands, acc):
    rows, half = operands[0].shape
    rows = rows // 2
    whole = pl.BlockSpec(memory_space=pltpu.VMEM)
    shape = jax.ShapeDtypeStruct((16, rows // 2, 2 * rows), jnp.float32)
    return pl.pallas_call(
        lambda *refs: gram_kernel(bool(acc), *refs),
        in_specs=[pl.BlockSpec(memory_space=pltpu.SMEM)] + [whole] * (len(operands) + len(acc)),
        out_specs=[whole, whole],
        out_shape=[shape, shape],
        scratch_shapes=[pltpu.VMEM((6 * rows, 2 * half), BF)],
        cost_estimate=cost(1000, 8 << 20),
        compiler_params=params(),
    )(info, *operands, *acc)


def to_four(pieces, axis):
    total = pieces[0].astype(jnp.float32)
    for d in (1, 2, 3):
        came = lax.ppermute(pieces[d], axis, [(i, (i + d) % 4) for i in range(4)])
        total = total + came.astype(jnp.float32)
    return total * 0.25


def after(value, *others):
    return lax.optimization_barrier((value, others))[0]


def along_y(own):
    nxt = lax.ppermute(own, "y", [((i + 1) % 4, i) for i in range(4)])
    last = lax.ppermute(own, "y", [(i, (i + 1) % 4) for i in range(4)])
    return nxt, last


def siblings(own, nxt, last):
    part = own.shape[0] // 2
    own_s = lax.ppermute(own, "core", SWAP)
    nxt_s = lax.ppermute(nxt[part:], "core", SWAP)
    last_s = lax.ppermute(last, "core", SWAP)
    return own, own_s, nxt, nxt_s, last, last_s


def gram_operands(keep, keep_y, other, other_y):
    return [
        array for pair in zip(siblings(keep, *keep_y), siblings(other, *other_y)) for array in pair
    ]


def mean_of_four(pieces):
    return jnp.sum(pieces.astype(jnp.float32), axis=0) * 0.25


def body(adjoint, courant, detector, sources, emission):
    groups, rows, width = adjoint.shape
    core = lax.axis_index("core")
    xl = lax.axis_index("xl")
    y = lax.axis_index("y")
    z = lax.axis_index("z")
    tile = lax.axis_index(GRID)
    first_cell = tile * rows * width
    xpos = lax.axis_index(XS)
    info = jnp.stack([core, xl, first_cell, y, xpos, z]).astype(jnp.int32)
    count = lax.axis_size(GRID)
    forward = [(i, i + 1) for i in range(count - 1)]
    backward = [(i + 1, i) for i in range(count - 1)]

    top, bottom = edges(adjoint, courant)
    up = lax.ppermute(bottom, GRID, forward)
    down = lax.ppermute(top, GRID, backward)
    columns = jnp.arange(width)

    def weights(c):
        return jnp.stack([
            c[0],
            c[1],
            jnp.where(columns == width - 1, 0.0, c[2]),
            jnp.where(columns == 0, 0.0, c[3]),
            1.0 - (c[0] + c[1] + c[2] + c[3]),
        ])

    local = sources - first_cell
    by_row = jnp.where(
        (local // width)[None, :] == jnp.arange(rows)[:, None], emission[None, :], 0.0
    )
    by_col = ((local % width)[:, None] == columns[None, :]).astype(jnp.float32)
    emis = jnp.dot(by_row, by_col, precision=lax.Precision.HIGHEST)
    det = detector[:, None]

    weights_in = weights(courant)
    mid, keep, send = stencil(
        inner_kernel, after(info, top, bottom), adjoint, [], weights_in, emis, det, [], INNER
    )
    other = lax.ppermute(send, "xl", SWAP)
    keep_y = along_y(after(keep, up, down))
    other_y = along_y(after(other, keep_y))
    totals = partial_gram(info, gram_operands(keep, keep_y, other, other_y), [])

    extended = jnp.concatenate(
        [edge_weights(up, groups), courant, edge_weights(down, groups)], axis=1
    )
    field, keep, send = stencil(
        outer_kernel, after(info, keep_y), adjoint, [up, down], weights(extended), emis, det,
        [mid], OUTER
    )
    other = lax.ppermute(send, "xl", SWAP)
    keep_y = along_y(keep)
    other_y = along_y(after(other, keep_y, totals))
    totals = partial_gram(info, gram_operands(keep, keep_y, other, other_y), totals)

    along_z, along_x = [
        (total * LIFT).astype(HALF).reshape(4, 4, groups // 4, groups) for total in totals
    ]
    along_x = to_four(along_x, XS).astype(HALF)
    along_z = to_four(along_z, "z").astype(HALF)
    along_x = mean_of_four(lax.all_to_all(along_x, "z", 0, 0, tiled=True))
    along_z = to_four(along_z, XS)
    moves = [((i + 2) % 4 * 4 + i, (i + 1) % 4 * 4 + (i + 3) % 4) for i in range(4)]
    halves = []
    for part in (along_z, along_x):
        moved = lax.ppermute(part.astype(HALF), ("z", "y"), moves).astype(jnp.float32)
        halves.append(jnp.where(lax.rem(y + 2, 4) == z, moved, part))
    summed = jnp.concatenate(halves, axis=0)
    total_sources = sources.shape[0] * count
    return field, summed * jnp.float32(16.0 / (LIFT * total_sources))


def solution(mesh):
    fine = Mesh(mesh.devices.reshape(4, 2, 2, 4, 2), ("z", "xh", "core", "y", "xl"))
    rec = ("y", "xl")
    in_specs = (P(rec, GRID, None), P(None, GRID, None), P(rec), P(GRID), P(GRID))
    out_specs = (P(rec, GRID, None), P(GRID, rec))
    return jax.shard_map(body, mesh=fine, in_specs=in_specs, out_specs=out_specs, check_vma=False)
```
